32 devices in a mesh: gy: 4 (over z), gx: 8 (over y, x, core).
Axes of the slice: x: 2, y: 2, z: 4, core: 2. Of those that a mesh axis runs over, the one named last changes fastest.
Arguments:
- mask: float32 [160, 1024], P('gy', 'gx'), may hold values from 0 to 1
- target: int32 [160, 1024], P('gy', 'gx'), may hold values 0 or 1
- kernels: bfloat16 [24, 35, 35], replicated, may hold values from -0.15625 to 0.15625
- offsets: int32 [8, 2], replicated, may hold values from -8 to 8, as said below
- load_weights: float32 [8], replicated, may hold values from 0.2 to 1
Outputs:
- update: float32 [160, 1024], P('gy', 'gx')
- loss: float32 [], replicated
The draws below stay inside these ranges and needn't reach their ends.
Inputs may be any that keep to these rules, and one draw needn't show every extreme that they name: `offsets`: some offset has row component 8 and some has column component -8.
All inputs are finite; a program needn't handle non-finite values. No bound on the sum of `target` on one device may be relied on, other than what follows from the above.
Results may differ from the reference program's by a relative error of at most 0.002.
Values may be sent and summed in bfloat16 or wider, within the bound.
No kernel may reach another device: no remote copies, remote signals or barrier semaphores. Data moves between devices by JAX's collectives and lax.ppermute only.
A program may use at most 64 MiB of HBM per device.

```python
import math
import jax
import jax.numpy as jnp
from jax import lax

KERNELS = 12
TAPS = 35
REACH = 8
LOAD_TAPS = 8
ROWS = 160
COLS = 1024


def draw_offsets(key, part):
    drawn = jax.random.randint(jax.random.fold_in(key, 11), (LOAD_TAPS, 2), -REACH, REACH + 1)
    drawn = drawn.at[0, 0].set(REACH)
    drawn = drawn.at[1, 1].set(-REACH)
    return drawn.astype(jnp.int32)


def with_ends(entries, rng, least, top_value):
    dims = entries.shape
    place = [jax.random.randint(jax.random.fold_in(rng, axis), (), 0, dims[axis]) for axis in range(len(dims))]
    entries = entries.at[tuple(place)].set(least)
    longest = dims.index(max(dims))
    place[longest] = (place[longest] + 1) % dims[longest]
    return entries.at[tuple(place)].set(top_value)


def level_of(key, dims, shards, low, top_value):
    level = 1.0
    for dim, shards_of in shards:
        steps = jax.random.uniform(jax.random.fold_in(jax.random.fold_in(key, 6), dim), (shards_of,), jnp.float32, low / len(shards), top_value / len(shards))
        level = level * jnp.repeat(jnp.exp(steps), dims[dim] // shards_of).reshape((-1,) + (1,) * (len(dims) - 1 - dim))
    return level


def centred(stream_key, dims, deviation, most, kind=jnp.bfloat16):
    return jnp.clip(deviation * jax.random.normal(stream_key, dims, jnp.float32), -most, most).astype(kind)


def setup_inputs(seed: int = 0) -> dict:
    key_list = jax.random.split(jax.random.key(seed), 6)
    mask = jnp.clip(1.0 * jax.random.uniform(key_list[0], (ROWS, COLS), jnp.float32) ** level_of(key_list[0], (ROWS, COLS), ((0, 4), (1, 8)), -0.2, 0.2), 0.0, 1.0)
    target = with_ends((jax.random.randint(key_list[1], (ROWS, COLS), 0, 2) < 1).astype(jnp.int32), jax.random.fold_in(key_list[1], 1), 0, 1)
    kernels = centred(key_list[2], (2 * KERNELS, TAPS, TAPS), (TAPS * TAPS) ** -0.5, 0.15625)
    offsets = draw_offsets(jax.random.fold_in(key_list[5], 71), 0)
    load_weights = jnp.clip(jnp.exp(jax.random.uniform(key_list[4], (LOAD_TAPS,), jnp.float32, math.log(0.2), math.log(1.0))), 0.2, 1.0)
    return {"mask": mask, "target": target, "kernels": kernels, "offsets": offsets, "load_weights": load_weights}


SMOOTH_TAPS = (0.0625, 0.25, 0.375, 0.25, 0.0625)
SHARPNESS = 4.0
THRESHOLD = 0.65
LOADING_GAIN = 0.5

def smooth_same(values):
    padded = jnp.pad(values, 2)
    height, width = values.shape
    partial_rows = sum((SMOOTH_TAPS[a] * padded[a:a + height, :] for a in range(5)))
    return sum((SMOOTH_TAPS[b] * partial_rows[:, b:b + width] for b in range(5)))

def correlate(field, weights, radius):
    return lax.conv_general_dilated(field[None], weights, (1, 1), [(radius, radius), (radius, radius)], dimension_numbers=('NCHW', 'OIHW', 'NCHW'), precision=lax.Precision.HIGHEST)[0]

def reference(mask, target, kernels, offsets, load_weights):
    height, width = mask.shape
    radius = kernels.shape[-1] // 2
    plane = mask.astype(jnp.bfloat16).astype(jnp.float32)
    forward_weights = kernels.astype(jnp.float32)[:, None]
    field = correlate(plane[None], forward_weights, radius)
    intensity = lax.optimization_barrier(jnp.sum(field * field, axis=0)) / KERNELS
    dense = smooth_same(intensity)
    develop = jax.nn.sigmoid(SHARPNESS * (dense - THRESHOLD))
    padded = jnp.pad(develop, REACH)
    loading = jnp.zeros((height, width), jnp.float32)
    for index in range(LOAD_TAPS):
        start_row = (REACH + offsets[index, 0]).astype(jnp.int32)
        start_col = (REACH + offsets[index, 1]).astype(jnp.int32)
        loading = loading + load_weights[index] * lax.dynamic_slice(padded, (start_row, start_col), (height, width))
    printed = develop - LOADING_GAIN / LOAD_TAPS * loading
    row_pos = jnp.arange(height, dtype=jnp.float32)
    col_pos = jnp.arange(width, dtype=jnp.float32)
    weight = (1.0 + 2.0 * row_pos / height)[:, None] * (1.0 + 2.0 * col_pos / width)[None, :]
    diff = printed - target.astype(jnp.float32)
    loss = jnp.sum(weight * diff * diff)
    resid = 2.0 * weight * diff
    resid_pad = jnp.pad(resid, REACH)
    back = jnp.zeros((height, width), jnp.float32)
    for index in range(LOAD_TAPS):
        start_row = (REACH - offsets[index, 0]).astype(jnp.int32)
        start_col = (REACH - offsets[index, 1]).astype(jnp.int32)
        back = back + load_weights[index] * lax.dynamic_slice(resid_pad, (start_row, start_col), (height, width))
    slope = resid - LOADING_GAIN / LOAD_TAPS * back
    dense_grad = slope * SHARPNESS * develop * (1.0 - develop)
    inten_grad = smooth_same(dense_grad)
    products = lax.optimization_barrier((2.0 * field * inten_grad / KERNELS).astype(jnp.bfloat16)).astype(jnp.float32)
    adjoint_weights = jnp.transpose(forward_weights[:, :, ::-1, ::-1], (1, 0, 2, 3))
    gradient = correlate(products, adjoint_weights, radius)[0]
    scale = jnp.sqrt(jnp.sum(gradient * gradient) / (height * width) + 1e-06)
    update = mask - gradient / scale
    return (update, loss)
```

```python
import functools

import jax
import jax.numpy as jnp
from jax import lax
from jax.experimental import pallas as pl
from jax.experimental.pallas import tpu as pltpu
from jax.sharding import PartitionSpec as P

REACH = 8
LOAD_TAPS = 8
SMOOTH = 2
SMOOTH_TAPS = (0.0625, 0.25, 0.375, 0.25, 0.0625)
SHARPNESS = 4.0
THRESHOLD = 0.65
LOADING_GAIN = 0.5

LANES = 128
WINDOW = 64
SLOT = 32
WIDE = 256
TOP = 24
PAD = 8

NT = (((1,), (1,)), ((), ()))
NN = (((1,), (0,)), ((), ()))
VMEM = pl.BlockSpec(memory_space=pltpu.VMEM)
SMEM = pl.BlockSpec(memory_space=pltpu.SMEM)


class Plan:
    def __init__(self, tile_rows, tile_cols, ny, nx, channels, taps):
        self.tile_rows, self.tile_cols, self.ny, self.nx = tile_rows, tile_cols, ny, nx
        self.rows, self.cols = tile_rows * ny, tile_cols * nx
        self.channels, self.taps, self.radius = channels, taps, taps // 2
        self.step = WINDOW - taps + 1
        self.field_halo = self.radius + 2 * (REACH + SMOOTH)
        self.halo = self.field_halo + self.radius
        self.blocks = -(-(tile_cols + 2 * self.field_halo) // self.step)
        self.pairs = -(-taps // 2)
        self.pairs += self.pairs % 2
        self.depth = self.pairs * LANES
        self.wide = channels * SLOT
        self.lo = self.field_halo - self.radius
        self.hi = self.field_halo + tile_cols + self.radius
        first, last = self.lo // self.step, (self.hi - 1) // self.step
        shift = self.field_halo + self.radius
        pieces = []
        for block in range(first, last + 1):
            low = max(0, shift - block * self.step)
            high = min(WINDOW, shift + tile_cols - block * self.step)
            pieces.append([block, block - first, block * self.step - shift, low, high])
        start = self.lo - first * self.step
        end = self.hi - last * self.step
        self.merged = (
            last > first
            and end <= start
            and end - 1 + taps - 1 < pieces[0][3]
            and start >= pieces[-1][4]
        )
        if self.merged:
            pieces[-1][1] = 0
        self.pieces = pieces
        self.operand_blocks = max(p[1] for p in pieces) + 1
        self.acc_rows = self.rows + 8 * ((self.pairs // 2 + 1) // 2) + 8


def roll_lanes(value, shift):
    return pltpu.roll(value, shift % value.shape[1], 1)


def lane_index(rows, lanes):
    return lax.broadcasted_iota(jnp.int32, (rows, lanes), 1)


def shifted_image(ref, rows, down, right):
    start = PAD + down
    rest = lax.rem(start, 8)
    base = pl.multiple_of(start - rest, 8)
    tiles = ref[pl.ds(base, rows + 8), :].reshape(rows // 8 + 1, 8, WIDE)
    tiles = pltpu.roll(tiles, lax.rem(8 - rest, 8), 1)
    row = lax.broadcasted_iota(jnp.int32, (rows // 8, 8, WIDE), 1)
    value = jnp.where(row < 8 - rest, tiles[:-1], tiles[1:]).reshape(rows, WIDE)
    return pltpu.roll(value, lax.rem(WIDE - right, WIDE), 1)


def strip_kernel(plan, *refs):
    pieces, out, hold = refs[: plan.ny], refs[plan.ny], refs[plan.ny + 1]
    here = lax.axis_index("gy")
    tile_rows, rows = plan.tile_rows, plan.rows
    for index, piece in enumerate(pieces):
        source = partner(here, index, plan.ny)
        value = piece[...].astype(jnp.float32)
        start = pl.multiple_of(source * tile_rows, 8)
        hold[0, pl.ds(start, tile_rows), :] = value[:tile_rows]
        hold[1, pl.ds(start, tile_rows), :] = value[tile_rows:]
    out[0:rows, :] = hold[0].astype(jnp.bfloat16)
    out[rows : 2 * rows, :] = hold[1].astype(jnp.bfloat16)


def build_bands(plan, taps_ref, bands):
    def channel(c, _):
        for q in range(plan.pairs):
            row = taps_ref[pl.ds(c * plan.pairs + q, 1), :]
            wide = jnp.broadcast_to(row, (SLOT, LANES))
            rolled = pltpu.roll(wide, 0, 1, stride=1, stride_axis=0)
            bands[pl.ds(pl.multiple_of(c * SLOT, SLOT), SLOT), q * LANES : (q + 1) * LANES] = (
                rolled.astype(jnp.bfloat16)
            )
        return 0

    lax.fori_loop(0, plan.channels, channel, 0)


def smooth_rows(ref, rows):
    total = None
    for a in range(5):
        term = SMOOTH_TAPS[a] * ref[pl.ds(PAD + a - 2, rows), :]
        total = term if total is None else total + term
    return total


def smooth_cols(value):
    total = None
    for b in range(5):
        term = SMOOTH_TAPS[b] * (value if b == 2 else roll_lanes(value, 2 - b))
        total = term if total is None else total + term
    return total


def main_kernel(
    plan,
    offsets,
    load_weights,
    own,
    near,
    far,
    taps_ref,
    grad_out,
    sums_out,
    bands,
    extended,
    turned,
    pairs_ref,
    patches,
    field,
    image,
    products,
    even,
    odd,
    tall,
):
    rows, tile_cols, step = plan.rows, plan.tile_cols, plan.step
    here = lax.axis_index("gx")
    first_col = here * tile_cols
    build_bands(plan, taps_ref, bands)

    is_even = here % 2 == 0
    lane = lane_index(rows, WIDE)
    blank = jnp.zeros((rows, LANES), jnp.float32)
    spread = []
    for part in range(2):
        mine, close, remote = (
            ref[part * rows : (part + 1) * rows, :].astype(jnp.float32)
            for ref in (own, near, far)
        )
        left = jnp.where(is_even, remote, close)
        right = jnp.where(is_even, close, remote)
        left, mid, right = (jnp.concatenate([v, blank], axis=1) for v in (left, mine, right))
        halo = plan.halo
        left = roll_lanes(left, halo - tile_cols)
        mid = roll_lanes(mid, halo)
        right = roll_lanes(right, halo + tile_cols)
        joined = jnp.where(lane < halo, left, jnp.where(lane < halo + tile_cols, mid, right))
        spread.append(jnp.where(lane < tile_cols + 2 * halo, joined, 0.0))
    tall_rows = extended.shape[0]
    extended[0:TOP, :] = jnp.zeros((TOP, WIDE), jnp.float32)
    extended[TOP : TOP + rows, :] = spread[0]
    extended[TOP + rows : tall_rows, :] = jnp.zeros((tall_rows - TOP - rows, WIDE), jnp.float32)
    target = roll_lanes(spread[1], -plan.radius)

    body_rows = tall_rows - 8
    half = lane_index(body_rows, LANES) < WINDOW
    for block in range(plan.blocks):
        window = roll_lanes(extended[...], -block * step)[:, :LANES]
        turned[...] = roll_lanes(window, WINDOW)
        pairs_ref[0:body_rows, :] = jnp.where(half, window[0:body_rows], turned[1 : body_rows + 1, :])
        for q in range(plan.pairs):
            start = TOP - plan.radius + 2 * q
            patches[block * rows : (block + 1) * rows, q * LANES : (q + 1) * LANES] = pairs_ref[
                start : start + rows, :
            ].astype(jnp.bfloat16)

    field[...] = lax.dot_general(patches[...], bands[...], NT, preferred_element_type=jnp.float32)

    col = lane + (first_col - plan.field_halo)
    inside = (col >= 0) & (col < plan.cols)
    total = jnp.zeros((rows, WIDE), jnp.float32)
    for block in range(plan.blocks):
        power = None
        for t in range(plan.wide // LANES):
            piece = field[block * rows : (block + 1) * rows, t * LANES : (t + 1) * LANES]
            power = piece * piece if power is None else power + piece * piece
        power = power + roll_lanes(power, 2 * SLOT)
        power = power + roll_lanes(power, SLOT)
        power = roll_lanes(jnp.concatenate([power, power], axis=1), block * step)
        total = jnp.where((lane >= block * step) & (lane < (block + 1) * step), power, total)
    kernels_count = plan.channels // 2
    intensity = jnp.where(inside, total / kernels_count, 0.0)
    zeros = jnp.zeros((PAD, WIDE), jnp.float32)
    image[0:PAD, :] = zeros
    image[PAD + rows : 3 * PAD + rows, :] = jnp.concatenate([zeros, zeros], axis=0)
    image[PAD : PAD + rows, :] = intensity
    dense = smooth_cols(smooth_rows(image, rows))
    develop = jnp.where(inside, jax.nn.sigmoid(SHARPNESS * (dense - THRESHOLD)), 0.0)

    image[PAD : PAD + rows, :] = develop
    loading = jnp.zeros((rows, WIDE), jnp.float32)
    for index in range(LOAD_TAPS):
        shifted = shifted_image(image, rows, offsets[index, 0], offsets[index, 1])
        loading = loading + load_weights[index] * shifted
    printed = develop - LOADING_GAIN / LOAD_TAPS * loading
    row_pos = lax.broadcasted_iota(jnp.int32, (rows, WIDE), 0).astype(jnp.float32)
    weight = (1.0 + 2.0 * row_pos / rows) * (1.0 + 2.0 * col.astype(jnp.float32) / plan.cols)
    diff = printed - target
    weighted = weight * diff
    mine = (lane >= plan.field_halo) & (lane < plan.field_halo + tile_cols)
    loss = jnp.sum(jnp.where(mine, weighted * diff, 0.0))
    resid = jnp.where(inside, 2.0 * weighted, 0.0)

    image[PAD : PAD + rows, :] = resid
    back = jnp.zeros((rows, WIDE), jnp.float32)
    for index in range(LOAD_TAPS):
        shifted = shifted_image(image, rows, -offsets[index, 0], -offsets[index, 1])
        back = back + load_weights[index] * shifted
    slope = resid - LOADING_GAIN / LOAD_TAPS * back
    image[PAD : PAD + rows, :] = slope * SHARPNESS * develop * (1.0 - develop)
    inten_grad = smooth_cols(smooth_rows(image, rows)) * (2.0 / kernels_count)
    used = inside & (lane >= plan.lo) & (lane < plan.hi)
    inten_grad = jnp.where(used, inten_grad, 0.0)

    narrow = lane_index(rows, LANES) < step
    gains = {}
    for block, operand, _, _, _ in plan.pieces:
        part = jnp.where(narrow, roll_lanes(inten_grad, -block * step)[:, :LANES], 0.0)
        part = part + roll_lanes(part, SLOT)
        gains[block] = part + roll_lanes(part, 2 * SLOT)
    for operand in range(plan.operand_blocks):
        blocks = [p[0] for p in plan.pieces if p[1] == operand]
        for t in range(plan.wide // LANES):
            value = None
            for block in blocks:
                piece = field[block * rows : (block + 1) * rows, t * LANES : (t + 1) * LANES]
                piece = piece * gains[block]
                value = piece if value is None else value + piece
            products[operand * rows : (operand + 1) * rows, t * LANES : (t + 1) * LANES] = (
                value.astype(jnp.bfloat16)
            )

    even[...] = jnp.zeros_like(even)
    odd[...] = jnp.zeros_like(odd)
    for group in range(plan.pairs // 2):
        out = lax.dot_general(
            products[...],
            bands[:, group * 2 * LANES : (group + 1) * 2 * LANES],
            NN,
            preferred_element_type=jnp.float32,
        )
        held = odd if group % 2 else even
        start = 8 * (group // 2)
        for operand in range(plan.operand_blocks):
            base = operand * plan.acc_rows + start
            held[base : base + rows, :] += out[operand * rows : (operand + 1) * rows, :]

    lane = lane_index(plan.acc_rows, LANES)
    total = [None, None]
    for operand in range(plan.operand_blocks):
        base = operand * plan.acc_rows
        tall[8 : 8 + plan.acc_rows, :] = odd[base : base + plan.acc_rows, :]
        both = even[base : base + plan.acc_rows, :] + tall[4 : 4 + plan.acc_rows, :]
        tall[8 : 8 + plan.acc_rows, :] = both
        pair = both[:, :LANES] + tall[6 : 6 + plan.acc_rows, LANES:]
        for _, index, shift, low, high in plan.pieces:
            if index != operand:
                continue
            keep = (lane >= low + shift) & (lane < high + shift)
            for a in range(2):
                piece = jnp.where(keep, roll_lanes(pair, shift - a * WINDOW), 0.0)
                total[a] = piece if total[a] is None else total[a] + piece
    tall[8 : 8 + plan.acc_rows, 0:LANES] = total[0]
    tall[8 : 8 + plan.acc_rows, LANES:] = total[1]
    gradient = (
        tall[8 + plan.radius : 8 + plan.radius + rows, 0:LANES]
        + tall[7 + plan.radius : 7 + plan.radius + rows, LANES:]
    )
    square = jnp.sum(gradient * gradient)
    tall[0:rows, 0:LANES] = gradient
    start = pl.multiple_of(lax.axis_index("gy") * plan.tile_rows, 8)
    grad_out[...] = tall[pl.ds(start, plan.tile_rows), 0:LANES]
    sums_out[0:8, :] = jnp.broadcast_to(loss, (8, LANES))
    sums_out[8:16, :] = jnp.broadcast_to(square, (8, LANES))


def update_kernel(plan, mask, grad, *refs):
    *sums, update, loss = refs
    total = sums[0][...]
    for other in sums[1:]:
        total = total + other[...]
    scale = jnp.sqrt(total[8:9, :] / (plan.rows * plan.cols) + 1e-06)
    update[...] = mask[...] - (grad[...] / scale)[:, : plan.tile_cols]
    loss[...] = total[0:1, 0:1]


def partner(here, step, count):
    if count & (count - 1) == 0:
        return jnp.bitwise_xor(here, step)
    return lax.rem(here + step, count)


def fetch(value, axis, step, count):
    if count & (count - 1) == 0:
        pairs = [(i, i ^ step) for i in range(count)]
    else:
        pairs = [((i + step) % count, i) for i in range(count)]
    return lax.ppermute(value, axis, pairs)


def swap_neighbours(value, axis, count, first):
    pairs = []
    for i in range(first, count - 1, 2):
        pairs += [(i, i + 1), (i + 1, i)]
    return lax.ppermute(value, axis, pairs)


def sum_terms(value, axis, count):
    if count & (count - 1):
        return [lax.psum(value, axis)]
    terms, bit = [value], 1
    while bit < count:
        value = functools.reduce(jnp.add, terms)
        steps = (bit, 2 * bit, 3 * bit) if 2 * bit < count else (bit,)
        terms = [value] + [fetch(value, axis, s, count) for s in steps]
        bit *= 4 if len(steps) == 3 else 2
    return terms


def body(mask, target, kernels, offsets, load_weights):
    tile_rows, tile_cols = mask.shape
    ny, nx = lax.axis_size("gy"), lax.axis_size("gx")
    channels, taps = kernels.shape[0], kernels.shape[1]
    plan = Plan(tile_rows, tile_cols, ny, nx, channels, taps)
    rows = plan.rows

    def params(megabytes):
        return pltpu.CompilerParams(vmem_limit_bytes=megabytes * 1024 * 1024)

    both = jnp.concatenate([mask.astype(jnp.bfloat16), target.astype(jnp.bfloat16)], axis=0)
    both = jnp.pad(both, ((0, 0), (0, LANES - tile_cols)))
    pieces = [both] + [fetch(both, "gy", s, ny) for s in range(1, ny)]
    strip = pl.pallas_call(
        functools.partial(strip_kernel, plan),
        out_shape=jax.ShapeDtypeStruct((2 * rows, LANES), jnp.bfloat16),
        in_specs=[VMEM] * ny,
        out_specs=VMEM,
        scratch_shapes=[pltpu.VMEM((2, rows, LANES), jnp.float32)],
        name="strip",
    )(*pieces)
    near = swap_neighbours(strip, "gx", nx, 0)
    far = swap_neighbours(strip, "gx", nx, 1)

    tap_rows = jnp.pad(
        kernels.astype(jnp.float32), ((0, 0), (0, 2 * plan.pairs - taps), (0, WINDOW - taps))
    ).reshape(channels * plan.pairs, LANES)

    tall_rows = TOP + rows + 32
    grad, sums = pl.pallas_call(
        functools.partial(main_kernel, plan),
        out_shape=(
            jax.ShapeDtypeStruct((tile_rows, LANES), jnp.float32),
            jax.ShapeDtypeStruct((16, LANES), jnp.float32),
        ),
        in_specs=[SMEM, SMEM, VMEM, VMEM, VMEM, VMEM],
        out_specs=(VMEM, VMEM),
        scratch_shapes=[
            pltpu.VMEM((plan.wide, plan.depth), jnp.bfloat16),
            pltpu.VMEM((tall_rows, WIDE), jnp.float32),
            pltpu.VMEM((tall_rows, LANES), jnp.float32),
            pltpu.VMEM((tall_rows, LANES), jnp.float32),
            pltpu.VMEM((plan.blocks * rows, plan.depth), jnp.bfloat16),
            pltpu.VMEM((plan.blocks * rows, plan.wide), jnp.float32),
            pltpu.VMEM((rows + 3 * PAD, WIDE), jnp.float32),
            pltpu.VMEM((plan.operand_blocks * rows, plan.wide), jnp.bfloat16),
            pltpu.VMEM((plan.operand_blocks * plan.acc_rows, 2 * LANES), jnp.float32),
            pltpu.VMEM((plan.operand_blocks * plan.acc_rows, 2 * LANES), jnp.float32),
            pltpu.VMEM((plan.acc_rows + 16, 2 * LANES), jnp.float32),
        ],
        compiler_params=params(56),
        name="step",
    )(offsets, load_weights, strip, near, far, tap_rows)

    terms = sum_terms(sums, "gx", nx)
    update, loss = pl.pallas_call(
        functools.partial(update_kernel, plan),
        out_shape=(
            jax.ShapeDtypeStruct((tile_rows, tile_cols), jnp.float32),
            jax.ShapeDtypeStruct((1, 1), jnp.float32),
        ),
        in_specs=[VMEM] * (2 + len(terms)),
        out_specs=(VMEM, VMEM),
        name="update",
    )(mask, grad, *terms)
    return update, loss.reshape(())


def solution(mesh):
    return jax.shard_map(
        body,
        mesh=mesh,
        in_specs=(P("gy", "gx"), P("gy", "gx"), P(), P(), P()),
        out_specs=(P("gy", "gx"), P()),
        check_vma=False,
    )
```

```python
import functools

import jax
import jax.numpy as jnp
from jax import lax
from jax.experimental import pallas as pl
from jax.experimental.pallas import tpu as pltpu
from jax.sharding import PartitionSpec as P

REACH = 8
LOAD_TAPS = 8
SMOOTH = 2
SMOOTH_TAPS = (0.0625, 0.25, 0.375, 0.25, 0.0625)
SHARPNESS = 4.0
THRESHOLD = 0.65
LOADING_GAIN = 0.5

LANES = 128
WINDOW = 64
SLOT = 32
WIDE = 256
TOP = 24
PAD = 8

NT = (((1,), (1,)), ((), ()))
NN = (((1,), (0,)), ((), ()))
VMEM = pl.BlockSpec(memory_space=pltpu.VMEM)
SMEM = pl.BlockSpec(memory_space=pltpu.SMEM)


class Plan:
    def __init__(self, tile_rows, tile_cols, ny, nx, channels, taps):
        self.tile_rows, self.tile_cols, self.ny, self.nx = tile_rows, tile_cols, ny, nx
        self.rows, self.cols = tile_rows * ny, tile_cols * nx
        self.channels, self.taps, self.radius = channels, taps, taps // 2
        self.step = WINDOW - taps + 1
        self.field_halo = self.radius + 2 * (REACH + SMOOTH)
        self.halo = self.field_halo + self.radius
        self.blocks = -(-(tile_cols + 2 * self.field_halo) // self.step)
        self.pairs = -(-taps // 2)
        self.pairs += self.pairs % 2
        self.depth = self.pairs * LANES
        self.wide = channels * SLOT
        self.lo = self.field_halo - self.radius
        self.hi = self.field_halo + tile_cols + self.radius
        first, last = self.lo // self.step, (self.hi - 1) // self.step
        shift = self.field_halo + self.radius
        pieces = []
        for block in range(first, last + 1):
            low = max(0, shift - block * self.step)
            high = min(WINDOW, shift + tile_cols - block * self.step)
            pieces.append([block, block - first, block * self.step - shift, low, high])
        start = self.lo - first * self.step
        end = self.hi - last * self.step
        self.merged = (
            last > first
            and end <= start
            and end - 1 + taps - 1 < pieces[0][3]
            and start >= pieces[-1][4]
        )
        if self.merged:
            pieces[-1][1] = 0
        self.pieces = pieces
        self.operand_blocks = max(p[1] for p in pieces) + 1
        low = sum(b * self.step < self.halo for b in range(self.blocks))
        end = self.halo + tile_cols
        high = sum(b * self.step + WINDOW > end for b in range(self.blocks))
        self.late = max(low, high)
        self.acc_rows = self.rows + 8 * ((self.pairs // 2 + 1) // 2) + 8


def roll_lanes(value, shift):
    return pltpu.roll(value, shift % value.shape[1], 1)


def lane_index(rows, lanes):
    return lax.broadcasted_iota(jnp.int32, (rows, lanes), 1)


def shifted_image(ref, rows, down, right):
    start = PAD + down
    rest = lax.rem(start, 8)
    base = pl.multiple_of(start - rest, 8)
    tiles = ref[pl.ds(base, rows + 8), :].reshape(rows // 8 + 1, 8, WIDE)
    tiles = pltpu.roll(tiles, lax.rem(8 - rest, 8), 1)
    row = lax.broadcasted_iota(jnp.int32, (rows // 8, 8, WIDE), 1)
    value = jnp.where(row < 8 - rest, tiles[:-1], tiles[1:]).reshape(rows, WIDE)
    return pltpu.roll(value, lax.rem(WIDE - right, WIDE), 1)


def pack_kernel(plan, mask, target, both, mask_out, target_in, sems):
    rows, cols = plan.tile_rows, plan.tile_cols
    copies = [
        pltpu.make_async_copy(source, held, sems.at[i])
        for i, (source, held) in enumerate(((mask, mask_out), (target, target_in)))
    ]
    for copy in copies:
        copy.start()
    if cols < LANES:
        both[...] = jnp.zeros_like(both)
    copies[0].wait()
    both[0:rows, 0:cols] = mask_out[...].astype(jnp.bfloat16)
    copies[1].wait()
    both[rows : 2 * rows, 0:cols] = target_in[...].astype(jnp.float32).astype(jnp.bfloat16)


def strip_kernel(plan, *refs):
    pieces, out, hold = refs[: plan.ny], refs[plan.ny + 1], refs[plan.ny + 2]
    here = lax.axis_index("gy")
    tile_rows, rows = plan.tile_rows, plan.rows
    for index, piece in enumerate(pieces):
        source = partner(here, index, plan.ny)
        value = piece[...].astype(jnp.float32)
        start = pl.multiple_of(source * tile_rows, 8)
        hold[0, pl.ds(start, tile_rows), :] = value[:tile_rows]
        hold[1, pl.ds(start, tile_rows), :] = value[tile_rows:]
    out[0:rows, :] = hold[0].astype(jnp.bfloat16)
    out[rows : 2 * rows, :] = hold[1].astype(jnp.bfloat16)


def bands_kernel(plan, kernels_ref, bands, row_ref, pairs_ref):
    channels, taps = plan.channels, plan.taps
    row_ref[...] = jnp.zeros_like(row_ref)
    for q in range(plan.pairs):
        for a in range(2):
            if 2 * q + a < taps:
                row_ref[a, :, 0:taps] = kernels_ref[2 * q + a].astype(jnp.float32)
            else:
                row_ref[a] = jnp.zeros((channels, LANES), jnp.float32)
        pairs_ref[q * channels : (q + 1) * channels, :] = row_ref[0] + roll_lanes(row_ref[1], WINDOW)

    def channel(c, _):
        for q in range(plan.pairs):
            row = pairs_ref[pl.ds(q * channels + c, 1), :]
            wide = jnp.broadcast_to(row, (SLOT, LANES))
            rolled = pltpu.roll(wide, 0, 1, stride=1, stride_axis=0)
            bands[pl.ds(pl.multiple_of(c * SLOT, SLOT), SLOT), q * LANES : (q + 1) * LANES] = (
                rolled.astype(jnp.bfloat16)
            )
        return 0

    lax.fori_loop(0, channels, channel, 0)


def smooth_rows(ref, rows):
    total = None
    for a in range(5):
        term = SMOOTH_TAPS[a] * ref[pl.ds(PAD + a - 2, rows), :]
        total = term if total is None else total + term
    return total


def smooth_cols(value):
    total = None
    for b in range(5):
        term = SMOOTH_TAPS[b] * (value if b == 2 else roll_lanes(value, 2 - b))
        total = term if total is None else total + term
    return total


def read_part(ref, part, rows):
    value = ref[part * rows : (part + 1) * rows, :].astype(jnp.float32)
    return jnp.concatenate([value, jnp.zeros((rows, LANES), jnp.float32)], axis=1)


def join_columns(plan, own, near, far, part):
    rows, tile_cols, halo = plan.rows, plan.tile_cols, plan.halo
    is_even = lax.axis_index("gx") % 2 == 0
    lane = lane_index(rows, WIDE)
    mid = roll_lanes(read_part(own, part, rows), halo)
    close = read_part(near, part, rows)
    remote = jnp.zeros_like(close) if far is None else read_part(far, part, rows)
    left = roll_lanes(jnp.where(is_even, remote, close), halo - tile_cols)
    right = roll_lanes(jnp.where(is_even, close, remote), halo + tile_cols)
    joined = jnp.where(lane < halo, left, jnp.where(lane < halo + tile_cols, mid, right))
    return jnp.where(lane < tile_cols + 2 * halo, joined, 0.0)


def fill_extended(plan, value, extended):
    rows, tall_rows = plan.rows, extended.shape[0]
    extended[0:TOP, :] = jnp.zeros((TOP, WIDE), jnp.float32)
    extended[TOP : TOP + rows, :] = value
    extended[TOP + rows : tall_rows, :] = jnp.zeros((tall_rows - TOP - rows, WIDE), jnp.float32)


def fill_patches(plan, block, index, extended, turned, pairs_ref, patches):
    rows, body_rows = plan.rows, extended.shape[0] - 8
    half = lane_index(body_rows, LANES) < WINDOW
    window = pltpu.roll(extended[...], lax.rem(WIDE - block * plan.step, WIDE), 1)[:, :LANES]
    turned[...] = roll_lanes(window, WINDOW)
    pairs_ref[0:body_rows, :] = jnp.where(half, window[0:body_rows], turned[1 : body_rows + 1, :])
    for q in range(plan.pairs):
        start = TOP - plan.radius + 2 * q
        patches[index * rows : (index + 1) * rows, q * LANES : (q + 1) * LANES] = pairs_ref[
            start : start + rows, :
        ].astype(jnp.bfloat16)


def early_kernel(plan, own, near, bands, field, extended, turned, pairs_ref, patches):
    rows, late, blocks = plan.rows, plan.late, plan.blocks
    fill_extended(plan, join_columns(plan, own, near, None, 0), extended)
    first = jnp.where(lax.axis_index("gx") % 2 == 0, late, 0)
    for index in range(blocks - late):
        fill_patches(plan, first + index, index, extended, turned, pairs_ref, patches)
    field[late * rows : blocks * rows, :] = lax.dot_general(
        patches[...], bands[...], NT, preferred_element_type=jnp.float32
    )


def late_kernel(
    plan,
    offsets,
    load_weights,
    own,
    near,
    far,
    bands,
    field_in,
    grad_out,
    sums_out,
    field,
    extended,
    turned,
    pairs_ref,
    patches,
    image,
    products,
    even,
    odd,
    tall,
):
    del field_in
    rows, tile_cols, step = plan.rows, plan.tile_cols, plan.step
    late, blocks = plan.late, plan.blocks
    here = lax.axis_index("gx")
    is_even = here % 2 == 0
    first_col = here * tile_cols
    lane = lane_index(rows, WIDE)
    fill_extended(plan, join_columns(plan, own, near, far, 0), extended)
    target = roll_lanes(join_columns(plan, own, near, far, 1), -plan.radius)
    first = jnp.where(is_even, 0, blocks - late)
    for index in range(late):
        fill_patches(plan, first + index, index, extended, turned, pairs_ref, patches)
    field[0 : late * rows, :] = lax.dot_general(
        patches[...], bands[...], NT, preferred_element_type=jnp.float32
    )

    def field_piece(block, t):
        slot = jnp.where(is_even, block, (block + late) % blocks)
        start = pl.multiple_of(slot * rows, 8)
        return field[pl.ds(start, rows), t * LANES : (t + 1) * LANES]

    col = lane + (first_col - plan.field_halo)
    inside = (col >= 0) & (col < plan.cols)
    total = jnp.zeros((rows, WIDE), jnp.float32)
    for block in range(plan.blocks):
        power = None
        for t in range(plan.wide // LANES):
            piece = field_piece(block, t)
            power = piece * piece if power is None else power + piece * piece
        power = power + roll_lanes(power, 2 * SLOT)
        power = power + roll_lanes(power, SLOT)
        power = roll_lanes(jnp.concatenate([power, power], axis=1), block * step)
        total = jnp.where((lane >= block * step) & (lane < (block + 1) * step), power, total)
    kernels_count = plan.channels // 2
    intensity = jnp.where(inside, total / kernels_count, 0.0)
    zeros = jnp.zeros((PAD, WIDE), jnp.float32)
    image[0:PAD, :] = zeros
    image[PAD + rows : 3 * PAD + rows, :] = jnp.concatenate([zeros, zeros], axis=0)
    image[PAD : PAD + rows, :] = intensity
    dense = smooth_cols(smooth_rows(image, rows))
    develop = jnp.where(inside, jax.nn.sigmoid(SHARPNESS * (dense - THRESHOLD)), 0.0)

    image[PAD : PAD + rows, :] = develop
    loading = jnp.zeros((rows, WIDE), jnp.float32)
    for index in range(LOAD_TAPS):
        shifted = shifted_image(image, rows, offsets[0, index], offsets[1, index])
        loading = loading + load_weights[index] * shifted
    printed = develop - LOADING_GAIN / LOAD_TAPS * loading
    row_pos = lax.broadcasted_iota(jnp.int32, (rows, WIDE), 0).astype(jnp.float32)
    weight = (1.0 + 2.0 * row_pos / rows) * (1.0 + 2.0 * col.astype(jnp.float32) / plan.cols)
    diff = printed - target
    weighted = weight * diff
    mine = (lane >= plan.field_halo) & (lane < plan.field_halo + tile_cols)
    loss = jnp.sum(jnp.where(mine, weighted * diff, 0.0))
    resid = jnp.where(inside, 2.0 * weighted, 0.0)

    image[PAD : PAD + rows, :] = resid
    back = jnp.zeros((rows, WIDE), jnp.float32)
    for index in range(LOAD_TAPS):
        shifted = shifted_image(image, rows, -offsets[0, index], -offsets[1, index])
        back = back + load_weights[index] * shifted
    slope = resid - LOADING_GAIN / LOAD_TAPS * back
    image[PAD : PAD + rows, :] = slope * SHARPNESS * develop * (1.0 - develop)
    inten_grad = smooth_cols(smooth_rows(image, rows)) * (2.0 / kernels_count)
    used = inside & (lane >= plan.lo) & (lane < plan.hi)
    inten_grad = jnp.where(used, inten_grad, 0.0)

    narrow = lane_index(rows, LANES) < step
    gains = {}
    for block, operand, _, _, _ in plan.pieces:
        part = jnp.where(narrow, roll_lanes(inten_grad, -block * step)[:, :LANES], 0.0)
        part = part + roll_lanes(part, SLOT)
        gains[block] = part + roll_lanes(part, 2 * SLOT)
    for operand in range(plan.operand_blocks):
        sources = [p[0] for p in plan.pieces if p[1] == operand]
        for t in range(plan.wide // LANES):
            value = None
            for block in sources:
                piece = field_piece(block, t) * gains[block]
                value = piece if value is None else value + piece
            products[operand * rows : (operand + 1) * rows, t * LANES : (t + 1) * LANES] = (
                value.astype(jnp.bfloat16)
            )

    even[...] = jnp.zeros_like(even)
    odd[...] = jnp.zeros_like(odd)
    for group in range(plan.pairs // 2):
        out = lax.dot_general(
            products[...],
            bands[:, group * 2 * LANES : (group + 1) * 2 * LANES],
            NN,
            preferred_element_type=jnp.float32,
        )
        held = odd if group % 2 else even
        start = 8 * (group // 2)
        for operand in range(plan.operand_blocks):
            base = operand * plan.acc_rows + start
            held[base : base + rows, :] += out[operand * rows : (operand + 1) * rows, :]

    lane = lane_index(plan.acc_rows, LANES)
    total = [None, None]
    for operand in range(plan.operand_blocks):
        base = operand * plan.acc_rows
        tall[8 : 8 + plan.acc_rows, :] = odd[base : base + plan.acc_rows, :]
        both = even[base : base + plan.acc_rows, :] + tall[4 : 4 + plan.acc_rows, :]
        tall[8 : 8 + plan.acc_rows, :] = both
        pair = both[:, :LANES] + tall[6 : 6 + plan.acc_rows, LANES:]
        for _, index, shift, low, high in plan.pieces:
            if index != operand:
                continue
            keep = (lane >= low + shift) & (lane < high + shift)
            for a in range(2):
                piece = jnp.where(keep, roll_lanes(pair, shift - a * WINDOW), 0.0)
                total[a] = piece if total[a] is None else total[a] + piece
    tall[8 : 8 + plan.acc_rows, 0:LANES] = total[0]
    tall[8 : 8 + plan.acc_rows, LANES:] = total[1]
    gradient = (
        tall[8 + plan.radius : 8 + plan.radius + rows, 0:LANES]
        + tall[7 + plan.radius : 7 + plan.radius + rows, LANES:]
    )
    square = jnp.sum(gradient * gradient)
    tall[0:rows, 0:LANES] = gradient
    start = pl.multiple_of(lax.axis_index("gy") * plan.tile_rows, 8)
    grad_out[...] = tall[pl.ds(start, plan.tile_rows), 0:LANES]
    sums_out[0:8, :] = jnp.broadcast_to(loss, (8, LANES))
    sums_out[8:16, :] = jnp.broadcast_to(square, (8, LANES))


def update_kernel(plan, mask, grad, *refs):
    *sums, update, loss = refs
    total = sums[0][...]
    for other in sums[1:]:
        total = total + other[...]
    scale = jnp.sqrt(total[8:9, :] / (plan.rows * plan.cols) + 1e-06)
    update[...] = mask[...] - (grad[...] / scale)[:, : plan.tile_cols]
    loss[...] = total[0:1, 0:1]


def partner(here, step, count):
    if count & (count - 1) == 0:
        return jnp.bitwise_xor(here, step)
    return lax.rem(here + step, count)


def fetch(value, axis, step, count):
    if count & (count - 1) == 0:
        pairs = [(i, i ^ step) for i in range(count)]
    else:
        pairs = [((i + step) % count, i) for i in range(count)]
    return lax.ppermute(value, axis, pairs)


def swap_neighbours(value, axis, count, first):
    pairs = []
    for i in range(first, count - 1, 2):
        pairs += [(i, i + 1), (i + 1, i)]
    return lax.ppermute(value, axis, pairs)


def sum_terms(value, axis, count):
    if count & (count - 1):
        return [lax.psum(value, axis)]
    terms, bit = [value], 1
    while bit < count:
        value = functools.reduce(jnp.add, terms)
        steps = (bit, 2 * bit, 3 * bit) if 2 * bit < count else (bit,)
        terms = [value] + [fetch(value, axis, s, count) for s in steps]
        bit *= 4 if len(steps) == 3 else 2
    return terms


def body(mask, target, kernels, offsets, load_weights):
    tile_rows, tile_cols = mask.shape
    ny, nx = lax.axis_size("gy"), lax.axis_size("gx")
    channels, taps = kernels.shape[0], kernels.shape[1]
    plan = Plan(tile_rows, tile_cols, ny, nx, channels, taps)
    rows = plan.rows

    def in_vmem(value):
        return pltpu.with_memory_space_constraint(value, pltpu.VMEM)

    def cost(nanoseconds):
        return pl.CostEstimate(flops=nanoseconds * 1000000, bytes_accessed=0, transcendentals=0)

    def params(scratch):
        return pltpu.CompilerParams(vmem_limit_bytes=scratch + 12 * 1024 * 1024)

    both, mask = pl.pallas_call(
        functools.partial(pack_kernel, plan),
        out_shape=(
            pltpu.VMEM((2 * tile_rows, LANES), jnp.bfloat16),
            pltpu.VMEM((tile_rows, tile_cols), jnp.float32),
        ),
        in_specs=[pl.BlockSpec(memory_space=pltpu.HBM)] * 2,
        out_specs=(VMEM,) * 2,
        scratch_shapes=[
            pltpu.VMEM((tile_rows, tile_cols), jnp.int32),
            pltpu.SemaphoreType.DMA((2,)),
        ],
        compiler_params=params(0),
        name="pack",
    )(*[pltpu.with_memory_space_constraint(v, pltpu.HBM) for v in (mask, target)])
    pieces = [both] + [fetch(both, "gy", s, ny) for s in range(1, ny)]

    bands = pl.pallas_call(
        functools.partial(bands_kernel, plan),
        out_shape=pltpu.VMEM((plan.wide, plan.depth), jnp.bfloat16),
        in_specs=[VMEM],
        out_specs=VMEM,
        scratch_shapes=[
            pltpu.VMEM((2, channels, LANES), jnp.float32),
            pltpu.VMEM((plan.pairs * channels, LANES), jnp.float32),
        ],
        compiler_params=params(0),
        cost_estimate=cost(2000),
        name="bands",
    )(in_vmem(jnp.transpose(kernels, (1, 0, 2))))
    bands = in_vmem(bands)
    strip = pl.pallas_call(
        functools.partial(strip_kernel, plan),
        out_shape=pltpu.VMEM((2 * rows, LANES), jnp.bfloat16),
        in_specs=[VMEM] * ny + [pl.BlockSpec(memory_space=pl.ANY)],
        out_specs=VMEM,
        scratch_shapes=[pltpu.VMEM((2, rows, LANES), jnp.float32)],
        compiler_params=params(0),
        cost_estimate=cost(300),
        name="strip",
    )(*[in_vmem(p) for p in pieces], bands)
    near = in_vmem(swap_neighbours(strip, "gx", nx, 0))
    far = in_vmem(swap_neighbours(strip, "gx", nx, 1))
    own = in_vmem(strip)

    tall_rows = TOP + rows + 32
    early = plan.blocks - plan.late
    patch_scratch = [
        pltpu.VMEM((tall_rows, WIDE), jnp.float32),
        pltpu.VMEM((tall_rows, LANES), jnp.float32),
        pltpu.VMEM((tall_rows, LANES), jnp.float32),
    ]
    field_type = pltpu.VMEM((plan.blocks * rows, plan.wide), jnp.float32)
    field = pl.pallas_call(
        functools.partial(early_kernel, plan),
        out_shape=field_type,
        in_specs=[VMEM] * 3,
        out_specs=VMEM,
        scratch_shapes=[
            *patch_scratch,
            pltpu.VMEM((early * rows, plan.depth), jnp.bfloat16),
        ],
        compiler_params=params(early * rows * plan.depth * 2),
        cost_estimate=cost(3500),
        name="early",
    )(own, near, bands)

    grad, sums, _ = pl.pallas_call(
        functools.partial(late_kernel, plan),
        out_shape=(
            pltpu.VMEM((tile_rows, LANES), jnp.float32),
            pltpu.VMEM((16, LANES), jnp.float32),
            field_type,
        ),
        in_specs=[SMEM, SMEM] + [VMEM] * 5,
        out_specs=(VMEM,) * 3,
        scratch_shapes=[
            *patch_scratch,
            pltpu.VMEM((plan.late * rows, plan.depth), jnp.bfloat16),
            pltpu.VMEM((rows + 3 * PAD, WIDE), jnp.float32),
            pltpu.VMEM((plan.operand_blocks * rows, plan.wide), jnp.bfloat16),
            pltpu.VMEM((plan.operand_blocks * plan.acc_rows, 2 * LANES), jnp.float32),
            pltpu.VMEM((plan.operand_blocks * plan.acc_rows, 2 * LANES), jnp.float32),
            pltpu.VMEM((plan.acc_rows + 16, 2 * LANES), jnp.float32),
        ],
        input_output_aliases={6: 2},
        compiler_params=params(
            plan.late * rows * plan.depth * 2
            + plan.operand_blocks * (rows * plan.wide * 2 + plan.acc_rows * 16 * LANES)
        ),
        cost_estimate=cost(12000),
        name="late",
    )(jnp.transpose(offsets), load_weights, own, near, far, bands, in_vmem(field))

    terms = [in_vmem(t) for t in sum_terms(sums, "gx", nx)]
    update, loss = pl.pallas_call(
        functools.partial(update_kernel, plan),
        out_shape=(
            jax.ShapeDtypeStruct((tile_rows, tile_cols), jnp.float32),
            jax.ShapeDtypeStruct((1, 1), jnp.float32),
        ),
        in_specs=[VMEM] * (2 + len(terms)),
        out_specs=(VMEM, VMEM),
        compiler_params=params(0),
        name="update",
    )(in_vmem(mask), in_vmem(grad), *terms)
    return update, loss.reshape(())


def solution(mesh):
    return jax.shard_map(
        body,
        mesh=mesh,
        in_specs=(P("gy", "gx"), P("gy", "gx"), P(), P(), P()),
        out_specs=(P("gy", "gx"), P()),
        check_vma=False,
    )
```

```python
import functools

import jax
import jax.numpy as jnp
from jax import lax
from jax.experimental import pallas as pl
from jax.experimental.pallas import tpu as pltpu
from jax.sharding import PartitionSpec as P

REACH = 8
LOAD_TAPS = 8
SMOOTH = 2
SMOOTH_TAPS = (0.0625, 0.25, 0.375, 0.25, 0.0625)
SHARPNESS = 4.0
THRESHOLD = 0.65
LOADING_GAIN = 0.5

LANES = 128
WINDOW = 64
SLOT = 32
WIDE = 256
TOP = 24
PAD = 8

NT = (((1,), (1,)), ((), ()))
NN = (((1,), (0,)), ((), ()))
VMEM = pl.BlockSpec(memory_space=pltpu.VMEM)
SMEM = pl.BlockSpec(memory_space=pltpu.SMEM)


class Plan:
    def __init__(self, tile_rows, tile_cols, ny, nx, channels, taps):
        self.tile_rows, self.tile_cols, self.ny, self.nx = tile_rows, tile_cols, ny, nx
        self.rows, self.cols = tile_rows * ny, tile_cols * nx
        self.channels, self.taps, self.radius = channels, taps, taps // 2
        self.step = WINDOW - taps + 1
        self.field_halo = self.radius + 2 * (REACH + SMOOTH)
        self.halo = self.field_halo + self.radius
        self.blocks = -(-(tile_cols + 2 * self.field_halo) // self.step)
        self.pairs = -(-taps // 2)
        self.pairs += self.pairs % 2
        self.depth = self.pairs * LANES
        self.wide = channels * SLOT
        self.lo = self.field_halo - self.radius
        self.hi = self.field_halo + tile_cols + self.radius
        first, last = self.lo // self.step, (self.hi - 1) // self.step
        shift = self.field_halo + self.radius
        pieces = []
        for block in range(first, last + 1):
            low = max(0, shift - block * self.step)
            high = min(WINDOW, shift + tile_cols - block * self.step)
            pieces.append([block, block - first, block * self.step - shift, low, high])
        start = self.lo - first * self.step
        end = self.hi - last * self.step
        self.merged = (
            last > first
            and end <= start
            and end - 1 + taps - 1 < pieces[0][3]
            and start >= pieces[-1][4]
        )
        if self.merged:
            pieces[-1][1] = 0
        self.pieces = pieces
        self.operand_blocks = max(p[1] for p in pieces) + 1
        low = sum(b * self.step < self.halo for b in range(self.blocks))
        end = self.halo + tile_cols
        high = sum(b * self.step + WINDOW > end for b in range(self.blocks))
        self.late = max(low, high)
        self.acc_rows = -(-(self.rows + taps) // 8) * 8


def roll_lanes(value, shift):
    return pltpu.roll(value, shift % value.shape[1], 1)


def lane_index(rows, lanes):
    return lax.broadcasted_iota(jnp.int32, (rows, lanes), 1)


def shifted_image(ref, rows, down, right):
    start = PAD + down
    rest = lax.rem(start, 8)
    base = pl.multiple_of(start - rest, 8)
    tiles = ref[pl.ds(base, rows + 8), :].reshape(rows // 8 + 1, 8, WIDE)
    tiles = pltpu.roll(tiles, lax.rem(8 - rest, 8), 1)
    row = lax.broadcasted_iota(jnp.int32, (rows // 8, 8, WIDE), 1)
    value = jnp.where(row < 8 - rest, tiles[:-1], tiles[1:]).reshape(rows, WIDE)
    return pltpu.roll(value, lax.rem(WIDE - right, WIDE), 1)


def pack_kernel(plan, mask, target, both, mask_out, target_in, sems):
    rows, cols = plan.tile_rows, plan.tile_cols
    copies = [
        pltpu.make_async_copy(source, held, sems.at[i])
        for i, (source, held) in enumerate(((mask, mask_out), (target, target_in)))
    ]
    for copy in copies:
        copy.start()
    if cols < LANES:
        both[...] = jnp.zeros_like(both)
    copies[0].wait()
    both[0:rows, 0:cols] = mask_out[...].astype(jnp.bfloat16)
    copies[1].wait()
    both[rows : 2 * rows, 0:cols] = target_in[...].astype(jnp.float32).astype(jnp.bfloat16)


def strip_kernel(plan, *refs):
    pieces, (out, facing, hold) = refs[: plan.ny], refs[plan.ny + 1 :]
    here = lax.axis_index("gy")
    tile_rows, rows = plan.tile_rows, plan.rows
    for index, piece in enumerate(pieces):
        source = partner(here, index, plan.ny)
        value = piece[...].astype(jnp.float32)
        start = pl.multiple_of(source * tile_rows, 8)
        hold[0, pl.ds(start, tile_rows), :] = value[:tile_rows]
        hold[1, pl.ds(start, tile_rows), :] = value[tile_rows:]
    out[0:rows, :] = hold[0].astype(jnp.bfloat16)
    out[rows : 2 * rows, :] = hold[1].astype(jnp.bfloat16)
    even = lax.axis_index("gx") % 2 == 0
    cols = plan.tile_cols
    first = jnp.where(even, hold[0], roll_lanes(hold[0], WINDOW - cols))
    second = jnp.where(even, roll_lanes(hold[1], WINDOW), roll_lanes(hold[1], LANES - cols))
    facing[...] = jnp.where(lane_index(rows, LANES) < WINDOW, first, second).astype(jnp.bfloat16)


def bands_kernel(plan, kernels_ref, bands, row_ref, pairs_ref):
    channels, taps = plan.channels, plan.taps
    row_ref[...] = jnp.zeros_like(row_ref)
    for q in range(plan.pairs):
        for a in range(2):
            if 2 * q + a < taps:
                row_ref[a, :, 0:taps] = kernels_ref[2 * q + a].astype(jnp.float32)
            else:
                row_ref[a] = jnp.zeros((channels, LANES), jnp.float32)
        pairs_ref[q * channels : (q + 1) * channels, :] = row_ref[0] + roll_lanes(row_ref[1], WINDOW)

    def channel(c, _):
        for q in range(plan.pairs):
            row = pairs_ref[pl.ds(q * channels + c, 1), :]
            wide = jnp.broadcast_to(row, (SLOT, LANES))
            rolled = pltpu.roll(wide, 0, 1, stride=1, stride_axis=0)
            bands[pl.ds(pl.multiple_of(c * SLOT, SLOT), SLOT), q * LANES : (q + 1) * LANES] = (
                rolled.astype(jnp.bfloat16)
            )
        return 0

    lax.fori_loop(0, channels, channel, 0)


def smooth_rows(ref, rows):
    total = None
    for a in range(5):
        term = SMOOTH_TAPS[a] * ref[pl.ds(PAD + a - 2, rows), :]
        total = term if total is None else total + term
    return total


def smooth_cols(value):
    total = None
    for b in range(5):
        term = SMOOTH_TAPS[b] * (value if b == 2 else roll_lanes(value, 2 - b))
        total = term if total is None else total + term
    return total


def widen(value):
    return jnp.concatenate([value, jnp.zeros_like(value)], axis=1)


def join_columns(plan, own, near, far, part):
    rows, tile_cols, halo = plan.rows, plan.tile_cols, plan.halo
    here = lax.axis_index("gx")
    even = here % 2 == 0
    lane = lane_index(rows, WIDE)
    mine, close = (
        widen(ref[part * rows : (part + 1) * rows, :].astype(jnp.float32)) for ref in (own, near)
    )
    mine = roll_lanes(mine, halo)
    to_right = halo + tile_cols
    close = pltpu.roll(close, jnp.where(even, to_right, WIDE + halo - tile_cols) % WIDE, 1)
    on_left, on_right = lane < halo, (lane >= to_right) & (lane < to_right + halo)
    joined = jnp.where((on_left & ~even) | (on_right & even), close, 0.0)
    joined = jnp.where((lane >= halo) & (lane < to_right), mine, joined)
    if far is not None:
        exists = jnp.where(even, here > 0, here < plan.nx - 1)
        shift = jnp.where(even, halo - WINDOW, to_right) + (WIDE - part * WINDOW)
        remote = pltpu.roll(widen(far[...].astype(jnp.float32)), shift % WIDE, 1)
        there = ((on_left & even) | (on_right & ~even)) & exists
        joined = jnp.where(there, remote, joined)
    return joined


def fill_extended(plan, value, extended):
    rows, tall_rows = plan.rows, extended.shape[0]
    extended[0:TOP, :] = jnp.zeros((TOP, WIDE), jnp.float32)
    extended[TOP : TOP + rows, :] = value
    extended[TOP + rows : tall_rows, :] = jnp.zeros((tall_rows - TOP - rows, WIDE), jnp.float32)


def fill_patches(plan, block, index, extended, turned, pairs_ref, patches):
    rows, body_rows = plan.rows, extended.shape[0] - 8
    half = lane_index(body_rows, LANES) < WINDOW
    window = pltpu.roll(extended[...], lax.rem(WIDE - block * plan.step, WIDE), 1)[:, :LANES]
    turned[...] = roll_lanes(window, WINDOW)
    pairs_ref[0:body_rows, :] = jnp.where(half, window[0:body_rows], turned[1 : body_rows + 1, :])
    for q in range(plan.pairs):
        start = TOP - plan.radius + 2 * q
        patches[index * rows : (index + 1) * rows, q * LANES : (q + 1) * LANES] = pairs_ref[
            start : start + rows, :
        ].astype(jnp.bfloat16)


def early_kernel(plan, own, near, bands, field, extended, turned, pairs_ref, patches):
    rows, late, blocks = plan.rows, plan.late, plan.blocks
    fill_extended(plan, join_columns(plan, own, near, None, 0), extended)
    first = jnp.where(lax.axis_index("gx") % 2 == 0, late, 0)
    for index in range(blocks - late):
        fill_patches(plan, first + index, index, extended, turned, pairs_ref, patches)
    field[late * rows : blocks * rows, :] = lax.dot_general(
        patches[...], bands[...], NT, preferred_element_type=jnp.float32
    )


def late_kernel(
    plan,
    offsets,
    load_weights,
    own,
    near,
    far,
    bands,
    field_in,
    grad_out,
    sums_out,
    field,
    extended,
    turned,
    pairs_ref,
    patches,
    image,
    products,
    low,
    high,
    tall,
):
    del field_in
    rows, tile_cols, step = plan.rows, plan.tile_cols, plan.step
    late, blocks = plan.late, plan.blocks
    here = lax.axis_index("gx")
    is_even = here % 2 == 0
    first_col = here * tile_cols
    lane = lane_index(rows, WIDE)
    fill_extended(plan, join_columns(plan, own, near, far, 0), extended)
    target = roll_lanes(join_columns(plan, own, near, far, 1), -plan.radius)
    first = jnp.where(is_even, 0, blocks - late)
    for index in range(late):
        fill_patches(plan, first + index, index, extended, turned, pairs_ref, patches)
    field[0 : late * rows, :] = lax.dot_general(
        patches[...], bands[...], NT, preferred_element_type=jnp.float32
    )

    def field_piece(block, t):
        slot = jnp.where(is_even, block, (block + late) % blocks)
        start = pl.multiple_of(slot * rows, 8)
        return field[pl.ds(start, rows), t * LANES : (t + 1) * LANES]

    col = lane + (first_col - plan.field_halo)
    inside = (col >= 0) & (col < plan.cols)
    total = jnp.zeros((rows, WIDE), jnp.float32)
    for block in range(plan.blocks):
        power = None
        for t in range(plan.wide // LANES):
            piece = field_piece(block, t)
            power = piece * piece if power is None else power + piece * piece
        power = power + roll_lanes(power, 2 * SLOT)
        power = power + roll_lanes(power, SLOT)
        power = roll_lanes(jnp.concatenate([power, power], axis=1), block * step)
        total = jnp.where((lane >= block * step) & (lane < (block + 1) * step), power, total)
    kernels_count = plan.channels // 2
    intensity = jnp.where(inside, total / kernels_count, 0.0)
    zeros = jnp.zeros((PAD, WIDE), jnp.float32)
    image[0:PAD, :] = zeros
    image[PAD + rows : 3 * PAD + rows, :] = jnp.concatenate([zeros, zeros], axis=0)
    image[PAD : PAD + rows, :] = intensity
    dense = smooth_cols(smooth_rows(image, rows))
    develop = jnp.where(inside, jax.nn.sigmoid(SHARPNESS * (dense - THRESHOLD)), 0.0)

    image[PAD : PAD + rows, :] = develop
    loading = jnp.zeros((rows, WIDE), jnp.float32)
    for index in range(LOAD_TAPS):
        shifted = shifted_image(image, rows, offsets[0, index], offsets[1, index])
        loading = loading + load_weights[index] * shifted
    printed = develop - LOADING_GAIN / LOAD_TAPS * loading
    row_pos = lax.broadcasted_iota(jnp.int32, (rows, WIDE), 0).astype(jnp.float32)
    weight = (1.0 + 2.0 * row_pos / rows) * (1.0 + 2.0 * col.astype(jnp.float32) / plan.cols)
    diff = printed - target
    weighted = weight * diff
    mine = (lane >= plan.field_halo) & (lane < plan.field_halo + tile_cols)
    loss = jnp.sum(jnp.where(mine, weighted * diff, 0.0))
    resid = jnp.where(inside, 2.0 * weighted, 0.0)

    image[PAD : PAD + rows, :] = resid
    back = jnp.zeros((rows, WIDE), jnp.float32)
    for index in range(LOAD_TAPS):
        shifted = shifted_image(image, rows, -offsets[0, index], -offsets[1, index])
        back = back + load_weights[index] * shifted
    slope = resid - LOADING_GAIN / LOAD_TAPS * back
    image[PAD : PAD + rows, :] = slope * SHARPNESS * develop * (1.0 - develop)
    inten_grad = smooth_cols(smooth_rows(image, rows)) * (2.0 / kernels_count)
    used = inside & (lane >= plan.lo) & (lane < plan.hi)
    inten_grad = jnp.where(used, inten_grad, 0.0)

    narrow = lane_index(rows, LANES) < step
    gains = {}
    for block, operand, _, _, _ in plan.pieces:
        begin, end = block * step // LANES, (block * step + step - 1) // LANES
        if begin == end:
            part = roll_lanes(
                inten_grad[:, begin * LANES : (begin + 1) * LANES], begin * LANES - block * step
            )
        else:
            part = roll_lanes(inten_grad, -block * step)[:, :LANES]
        part = jnp.where(narrow, part, 0.0)
        part = part + roll_lanes(part, SLOT)
        gains[block] = part + roll_lanes(part, 2 * SLOT)
    for operand in range(plan.operand_blocks):
        sources = [p[0] for p in plan.pieces if p[1] == operand]
        for t in range(plan.wide // LANES):
            value = None
            for block in sources:
                piece = field_piece(block, t) * gains[block]
                value = piece if value is None else value + piece
            lanes = slice(t * LANES, (t + 1) * LANES)
            products[operand * rows : (operand + 1) * rows, lanes] = value.astype(jnp.bfloat16)

    acc_rows, group_lanes = plan.acc_rows, 2 * LANES
    low[...] = jnp.zeros_like(low)
    high[...] = jnp.zeros_like(high)

    def add_groups(index, count):
        lanes = pl.ds(pl.multiple_of(index * 2 * group_lanes, LANES), count * group_lanes)
        out = lax.dot_general(
            products[...], bands[:, lanes], NN, preferred_element_type=jnp.float32
        )
        for operand in range(plan.operand_blocks):
            held = pl.ds(pl.multiple_of(operand * acc_rows + index * 8, 8), rows)
            block = slice(operand * rows, (operand + 1) * rows)
            low[held, :] += out[block, :group_lanes]
            if count == 2:
                high[held, :] += out[block, group_lanes:]

    def both_groups(index, carry):
        add_groups(index, 2)
        return carry

    groups = plan.pairs // 2
    lax.fori_loop(0, groups // 2, both_groups, 0)
    if groups % 2:
        add_groups(groups // 2, 1)

    start_row = plan.radius - 1
    count = -(-(rows + 1) // 8) * 8
    lane = lane_index(count, LANES)
    total = [None, None]
    for operand in range(plan.operand_blocks):
        base = operand * acc_rows + start_row
        pair = None
        for out, tap in ((low, 0), (low, 2), (high, 4), (high, 6)):
            lanes = slice(LANES, 2 * LANES) if tap % 4 else slice(0, LANES)
            piece = out[base - tap : base - tap + count, lanes]
            pair = piece if pair is None else pair + piece
        for _, index, shift, lowest, highest in plan.pieces:
            if index != operand:
                continue
            keep = (lane >= lowest + shift) & (lane < highest + shift)
            for a in range(2):
                piece = jnp.where(keep, roll_lanes(pair, shift - a * WINDOW), 0.0)
                total[a] = piece if total[a] is None else total[a] + piece
    tall[...] = total[0]
    gradient = tall[1 : 1 + rows, :] + total[1][:rows]
    square = jnp.sum(gradient * gradient)
    tall[0:rows, :] = gradient
    start = pl.multiple_of(lax.axis_index("gy") * plan.tile_rows, 8)
    grad_out[...] = tall[pl.ds(start, plan.tile_rows), :]
    sums_out[0:4, :] = jnp.broadcast_to(loss, (4, LANES))
    sums_out[4:8, :] = jnp.broadcast_to(square, (4, LANES))


def update_kernel(plan, mask, grad, *refs):
    *sums, update, loss = refs
    total = sums[0][...]
    for other in sums[1:]:
        total = total + other[...]
    scale = jnp.sqrt(total[4:5, :] / (plan.rows * plan.cols) + 1e-06)
    update[...] = mask[...] - (grad[...] / scale)[:, : plan.tile_cols]
    loss[...] = total[0:1, 0:1]


def partner(here, step, count):
    if count & (count - 1) == 0:
        return jnp.bitwise_xor(here, step)
    return lax.rem(here + step, count)


def fetch(value, axis, step, count):
    if count & (count - 1) == 0:
        pairs = [(i, i ^ step) for i in range(count)]
    else:
        pairs = [((i + step) % count, i) for i in range(count)]
    return lax.ppermute(value, axis, pairs)


def swap_neighbours(value, axis, count, first):
    pairs = []
    for i in range(first, count - 1, 2):
        pairs += [(i, i + 1), (i + 1, i)]
    if first and count % 2 == 0:
        pairs += [(0, count - 1), (count - 1, 0)]
    return lax.ppermute(value, axis, pairs)


def sum_terms(value, axis, count):
    if count & (count - 1):
        return [lax.psum(value, axis)]
    terms, bit = [value], 1
    while bit < count:
        value = functools.reduce(jnp.add, terms)
        steps = (bit, 2 * bit, 3 * bit) if 2 * bit < count else (bit,)
        terms = [value] + [fetch(value, axis, s, count) for s in steps]
        bit *= 4 if len(steps) == 3 else 2
    return terms


def body(mask, target, kernels, offsets, load_weights):
    tile_rows, tile_cols = mask.shape
    ny, nx = lax.axis_size("gy"), lax.axis_size("gx")
    channels, taps = kernels.shape[0], kernels.shape[1]
    plan = Plan(tile_rows, tile_cols, ny, nx, channels, taps)
    rows = plan.rows

    def in_vmem(value):
        return pltpu.with_memory_space_constraint(value, pltpu.VMEM)

    def cost(nanoseconds):
        return pl.CostEstimate(flops=nanoseconds * 1000000, bytes_accessed=0, transcendentals=0)

    def params(scratch):
        return pltpu.CompilerParams(vmem_limit_bytes=scratch + 12 * 1024 * 1024)

    both, mask = pl.pallas_call(
        functools.partial(pack_kernel, plan),
        out_shape=(
            pltpu.VMEM((2 * tile_rows, LANES), jnp.bfloat16),
            pltpu.VMEM((tile_rows, tile_cols), jnp.float32),
        ),
        in_specs=[pl.BlockSpec(memory_space=pltpu.HBM)] * 2,
        out_specs=(VMEM,) * 2,
        scratch_shapes=[
            pltpu.VMEM((tile_rows, tile_cols), jnp.int32),
            pltpu.SemaphoreType.DMA((2,)),
        ],
        compiler_params=params(0),
        name="pack",
    )(*[pltpu.with_memory_space_constraint(v, pltpu.HBM) for v in (mask, target)])
    pieces = [both] + [fetch(both, "gy", s, ny) for s in range(1, ny)]

    bands = pl.pallas_call(
        functools.partial(bands_kernel, plan),
        out_shape=pltpu.VMEM((plan.wide, plan.depth), jnp.bfloat16),
        in_specs=[VMEM],
        out_specs=VMEM,
        scratch_shapes=[
            pltpu.VMEM((2, channels, LANES), jnp.float32),
            pltpu.VMEM((plan.pairs * channels, LANES), jnp.float32),
        ],
        compiler_params=params(0),
        cost_estimate=cost(2000),
        name="bands",
    )(in_vmem(jnp.transpose(kernels, (1, 0, 2))))
    bands = in_vmem(bands)
    strip, facing = pl.pallas_call(
        functools.partial(strip_kernel, plan),
        out_shape=(
            pltpu.VMEM((2 * rows, LANES), jnp.bfloat16),
            pltpu.VMEM((rows, LANES), jnp.bfloat16),
        ),
        in_specs=[VMEM] * ny + [pl.BlockSpec(memory_space=pl.ANY)],
        out_specs=(VMEM,) * 2,
        scratch_shapes=[pltpu.VMEM((2, rows, LANES), jnp.float32)],
        compiler_params=params(0),
        cost_estimate=cost(300),
        name="strip",
    )(*[in_vmem(p) for p in pieces], bands)
    near = in_vmem(swap_neighbours(strip, "gx", nx, 0))
    far = in_vmem(swap_neighbours(facing, "gx", nx, 1))
    own = in_vmem(strip)

    tall_rows = TOP + rows + 32
    early = plan.blocks - plan.late
    patch_scratch = [
        pltpu.VMEM((tall_rows, WIDE), jnp.float32),
        pltpu.VMEM((tall_rows, LANES), jnp.float32),
        pltpu.VMEM((tall_rows, LANES), jnp.float32),
    ]
    field_type = pltpu.VMEM((plan.blocks * rows, plan.wide), jnp.float32)
    field = pl.pallas_call(
        functools.partial(early_kernel, plan),
        out_shape=field_type,
        in_specs=[VMEM] * 3,
        out_specs=VMEM,
        scratch_shapes=[
            *patch_scratch,
            pltpu.VMEM((early * rows, plan.depth), jnp.bfloat16),
        ],
        compiler_params=params(early * rows * plan.depth * 2),
        cost_estimate=cost(3500),
        name="early",
    )(own, near, bands)

    grad, sums, _ = pl.pallas_call(
        functools.partial(late_kernel, plan),
        out_shape=(
            pltpu.VMEM((tile_rows, LANES), jnp.float32),
            pltpu.VMEM((8, LANES), jnp.float32),
            field_type,
        ),
        in_specs=[SMEM, SMEM] + [VMEM] * 5,
        out_specs=(VMEM,) * 3,
        scratch_shapes=[
            *patch_scratch,
            pltpu.VMEM((plan.late * rows, plan.depth), jnp.bfloat16),
            pltpu.VMEM((rows + 3 * PAD, WIDE), jnp.float32),
            pltpu.VMEM((plan.operand_blocks * rows, plan.wide), jnp.bfloat16),
            pltpu.VMEM((plan.operand_blocks * plan.acc_rows, 2 * LANES), jnp.float32),
            pltpu.VMEM((plan.operand_blocks * plan.acc_rows, 2 * LANES), jnp.float32),
            pltpu.VMEM((-(-(rows + 1) // 8) * 8, LANES), jnp.float32),
        ],
        input_output_aliases={6: 2},
        compiler_params=params(
            plan.late * rows * plan.depth * 2
            + plan.operand_blocks * (rows * plan.wide * 2 + plan.acc_rows * 16 * LANES)
        ),
        cost_estimate=cost(12000),
        name="late",
    )(jnp.transpose(offsets), load_weights, own, near, far, bands, in_vmem(field))

    terms = [in_vmem(t) for t in sum_terms(sums, "gx", nx)]
    update, loss = pl.pallas_call(
        functools.partial(update_kernel, plan),
        out_shape=(
            jax.ShapeDtypeStruct((tile_rows, tile_cols), jnp.float32),
            jax.ShapeDtypeStruct((1, 1), jnp.float32),
        ),
        in_specs=[VMEM] * (2 + len(terms)),
        out_specs=(VMEM, VMEM),
        compiler_params=params(0),
        name="update",
    )(in_vmem(mask), in_vmem(grad), *terms)
    return update, loss.reshape(())


def solution(mesh):
    return jax.shard_map(
        body,
        mesh=mesh,
        in_specs=(P("gy", "gx"), P("gy", "gx"), P(), P(), P()),
        out_specs=(P("gy", "gx"), P()),
        check_vma=False,
    )
```

```python
import functools

import jax
import jax.numpy as jnp
from jax import lax
from jax.experimental import pallas as pl
from jax.experimental.pallas import tpu as pltpu
from jax.sharding import PartitionSpec as P

REACH = 8
LOAD_TAPS = 8
SMOOTH = 2
SMOOTH_TAPS = (0.0625, 0.25, 0.375, 0.25, 0.0625)
SHARPNESS = 4.0
THRESHOLD = 0.65
LOADING_GAIN = 0.5

LANES = 128
WINDOW = 64
SLOT = 32
WIDE = 256
TOP = 24
CHUNK = 32
PAD = 8

NT = (((1,), (1,)), ((), ()))
NN = (((1,), (0,)), ((), ()))
VMEM = pl.BlockSpec(memory_space=pltpu.VMEM)


class Plan:
    def __init__(self, tile_rows, tile_cols, ny, nx, channels, taps):
        self.tile_rows, self.tile_cols, self.ny, self.nx = tile_rows, tile_cols, ny, nx
        self.rows, self.cols = tile_rows * ny, tile_cols * nx
        self.channels, self.taps, self.radius = channels, taps, taps // 2
        self.step = WINDOW - taps + 1
        self.field_halo = self.radius + 2 * (REACH + SMOOTH)
        self.halo = self.field_halo + self.radius
        self.blocks = -(-(tile_cols + 2 * self.field_halo) // self.step)
        self.pairs = -(-taps // 2)
        self.pairs += self.pairs % 2
        self.depth = self.pairs * LANES
        self.wide = channels * SLOT
        self.lo = self.field_halo - self.radius
        self.hi = self.field_halo + tile_cols + self.radius
        first, last = self.lo // self.step, (self.hi - 1) // self.step
        shift = self.field_halo + self.radius
        pieces = []
        for block in range(first, last + 1):
            low = max(0, shift - block * self.step)
            high = min(WINDOW, shift + tile_cols - block * self.step)
            pieces.append([block, block - first, block * self.step - shift, low, high])
        start = self.lo - first * self.step
        end = self.hi - last * self.step
        self.merged = (
            last > first
            and end <= start
            and end - 1 + taps - 1 < pieces[0][3]
            and start >= pieces[-1][4]
        )
        if self.merged:
            pieces[-1][1] = 0
        self.pieces = pieces
        self.operand_blocks = max(p[1] for p in pieces) + 1
        low = sum(b * self.step < self.halo for b in range(self.blocks))
        end = self.halo + tile_cols
        high = sum(b * self.step + WINDOW > end for b in range(self.blocks))
        self.late = max(low, high)
        self.acc_rows = -(-(self.rows + taps) // 8) * 8


def roll_lanes(value, shift):
    return pltpu.roll(value, shift % value.shape[1], 1)


def lane_index(rows, lanes):
    return lax.broadcasted_iota(jnp.int32, (rows, lanes), 1)


def shifted_chunk(ref, start, down, right):
    rest = lax.rem(PAD + down, 8)
    base = pl.multiple_of(start + PAD + down - rest, 8)
    tiles = ref[pl.ds(base, CHUNK + 8), :].reshape(CHUNK // 8 + 1, 8, WIDE)
    tiles = pltpu.roll(tiles, lax.rem(8 - rest, 8), 1)
    row = lax.broadcasted_iota(jnp.int32, (CHUNK // 8, 8, WIDE), 1)
    value = jnp.where(row < 8 - rest, tiles[:-1], tiles[1:]).reshape(CHUNK, WIDE)
    return pltpu.roll(value, lax.rem(WIDE - right, WIDE), 1)


def pack_kernel(plan, mask, target, both, mask_out, target_in, sems):
    rows, cols = plan.tile_rows, plan.tile_cols
    copies = [
        pltpu.make_async_copy(source, held, sems.at[i])
        for i, (source, held) in enumerate(((mask, mask_out), (target, target_in)))
    ]
    for copy in copies:
        copy.start()
    if cols < LANES:
        both[...] = jnp.zeros_like(both)
    copies[0].wait()
    both[0:rows, 0:cols] = mask_out[...].astype(jnp.bfloat16)
    copies[1].wait()
    both[rows : 2 * rows, 0:cols] = target_in[...].astype(jnp.float32).astype(jnp.bfloat16)


def entries(row):
    column = lane_index(1, row.shape[1])
    return [jnp.sum(jnp.where(column == i, row, 0)) for i in range(row.shape[1])]


def strip_kernel(plan, *refs):
    pieces, (out, to_near, to_far, hold) = refs[: plan.ny], refs[plan.ny + 1 :]
    here = lax.axis_index("gy")
    tile_rows, rows = plan.tile_rows, plan.rows
    for index, piece in enumerate(pieces):
        source = partner(here, index, plan.ny)
        value = piece[...].astype(jnp.float32)
        start = pl.multiple_of(source * tile_rows, 8)
        hold[0, pl.ds(start, tile_rows), :] = value[:tile_rows]
        hold[1, pl.ds(start, tile_rows), :] = value[tile_rows:]
    out[0:rows, :] = hold[0].astype(jnp.bfloat16)
    out[rows : 2 * rows, :] = hold[1].astype(jnp.bfloat16)
    even = lax.axis_index("gx") % 2 == 0
    cols = plan.tile_cols
    first = lane_index(rows, LANES) < WINDOW
    low = jnp.where(first, hold[0], roll_lanes(hold[1], WINDOW))
    high = jnp.where(first, roll_lanes(hold[0], WINDOW - cols), roll_lanes(hold[1], LANES - cols))
    to_near[...] = jnp.where(even, high, low).astype(jnp.bfloat16)
    to_far[...] = jnp.where(even, low, high).astype(jnp.bfloat16)


def bands_kernel(plan, kernels_ref, bands, row_ref, pairs_ref):
    channels, taps = plan.channels, plan.taps
    row_ref[...] = jnp.zeros_like(row_ref)
    for q in range(plan.pairs):
        for a in range(2):
            if 2 * q + a < taps:
                row_ref[a, :, 0:taps] = kernels_ref[2 * q + a].astype(jnp.float32)
            else:
                row_ref[a] = jnp.zeros((channels, LANES), jnp.float32)
        pairs_ref[q * channels : (q + 1) * channels, :] = row_ref[0] + roll_lanes(row_ref[1], WINDOW)

    def channel(c, _):
        for q in range(plan.pairs):
            row = pairs_ref[pl.ds(q * channels + c, 1), :]
            wide = jnp.broadcast_to(row, (SLOT, LANES))
            rolled = pltpu.roll(wide, 0, 1, stride=1, stride_axis=0)
            bands[pl.ds(pl.multiple_of(c * SLOT, SLOT), SLOT), q * LANES : (q + 1) * LANES] = (
                rolled.astype(jnp.bfloat16)
            )
        return 0

    lax.fori_loop(0, channels, channel, 0)


def smooth_chunk(ref, start):
    rows = [chunk_at(ref, start, PAD + a) for a in (-2, -1, 0, 1, 2)]
    total = SMOOTH_TAPS[2] * rows[2]
    total = total + SMOOTH_TAPS[1] * (rows[1] + rows[3]) + SMOOTH_TAPS[0] * (rows[0] + rows[4])
    cols = [total if b == 0 else roll_lanes(total, -b) for b in (-2, -1, 0, 1, 2)]
    total = SMOOTH_TAPS[2] * cols[2]
    return total + SMOOTH_TAPS[1] * (cols[1] + cols[3]) + SMOOTH_TAPS[0] * (cols[0] + cols[4])


def widen(value):
    return jnp.concatenate([value, jnp.zeros_like(value)], axis=1)


def each_chunk(rows, work):
    count = rows // CHUNK
    if count <= 8:
        results = [work(i * CHUNK) for i in range(count)]
        return None if results[0] is None else functools.reduce(jnp.add, results)
    zero = jax.eval_shape(lambda: work(0))

    def step(index, total):
        result = work(pl.multiple_of(index * CHUNK, CHUNK))
        return None if result is None else total + result

    return lax.fori_loop(0, count, step, None if zero is None else jnp.zeros(zero.shape, zero.dtype))


def chunk_at(ref, start, offset):
    if isinstance(start, int):
        return ref[start + offset : start + offset + CHUNK, :]
    return ref[pl.ds(start, CHUNK + 2 * PAD), :][offset : offset + CHUNK]


def join_columns(plan, own, near, far, part, start):
    tile_cols, halo = plan.tile_cols, plan.halo
    here = lax.axis_index("gx")
    even = here % 2 == 0
    lane = lane_index(CHUNK, WIDE)
    to_right = halo + tile_cols
    on_left, on_right = lane < halo, (lane >= to_right) & (lane < to_right + halo)

    def side(ref, right):
        shift = jnp.where(right, to_right, halo - WINDOW) + (WIDE - part * WINDOW)
        value = widen(ref[pl.ds(start, CHUNK), :].astype(jnp.float32))
        return pltpu.roll(value, shift % WIDE, 1), (on_left & ~right) | (on_right & right)

    mine = widen(own[pl.ds(part * plan.rows + start, CHUNK), :].astype(jnp.float32))
    value, there = side(near, even)
    joined = jnp.where(there, value, 0.0)
    joined = jnp.where((lane >= halo) & (lane < to_right), roll_lanes(mine, halo), joined)
    if far is not None:
        value, there = side(far, ~even)
        exists = jnp.where(even, here > 0, here < plan.nx - 1)
        joined = jnp.where(there & exists, value, joined)
    return joined


def fill_extended(plan, own, near, far, extended):
    rows, tall_rows = plan.rows, extended.shape[0]
    extended[0:TOP, :] = jnp.zeros((TOP, WIDE), jnp.float32)
    extended[TOP + rows : tall_rows, :] = jnp.zeros((tall_rows - TOP - rows, WIDE), jnp.float32)

    def fill(start):
        extended[pl.ds(TOP + start, CHUNK), :] = join_columns(plan, own, near, far, 0, start)

    each_chunk(rows, fill)


def fill_patches(plan, block, index, extended, turned, pairs_ref, patches):
    rows, body_rows = plan.rows, extended.shape[0] - 8
    half = lane_index(body_rows, LANES) < WINDOW
    window = pltpu.roll(extended[...], lax.rem(WIDE - block * plan.step, WIDE), 1)[:, :LANES]
    turned[...] = roll_lanes(window, WINDOW)
    pairs_ref[0:body_rows, :] = jnp.where(half, window[0:body_rows], turned[1 : body_rows + 1, :])
    for q in range(8):
        start = TOP - plan.radius + 2 * q
        uses = range(q, plan.pairs, 8)
        height = rows + 16 * (len(uses) - 1)
        value = pairs_ref[start : start + height, :].astype(jnp.bfloat16)
        for tile, pair in enumerate(uses):
            patches[index * rows : (index + 1) * rows, pair * LANES : (pair + 1) * LANES] = value[
                16 * tile : 16 * tile + rows
            ]


def early_kernel(plan, own, near, bands, field, extended, turned, pairs_ref, patches):
    rows, late, blocks = plan.rows, plan.late, plan.blocks
    fill_extended(plan, own, near, None, extended)
    first = jnp.where(lax.axis_index("gx") % 2 == 0, late, 0)
    for index in range(blocks - late):
        fill_patches(plan, first + index, index, extended, turned, pairs_ref, patches)
    field[late * rows : blocks * rows, :] = lax.dot_general(
        patches[...], bands[...], NT, preferred_element_type=jnp.float32
    )


def late_kernel(
    plan,
    offsets,
    load_weights,
    own,
    near,
    far,
    bands,
    field_in,
    grad_out,
    sums_out,
    field,
    extended,
    turned,
    pairs_ref,
    patches,
    intensity,
    develop,
    resid,
    dense_grad,
    products,
    low,
    high,
    tall,
):
    del field_in
    downs, rights = (entries(offsets[axis : axis + 1, :]) for axis in range(2))
    load_gains = entries(load_weights[...] * (LOADING_GAIN / LOAD_TAPS))
    rows, tile_cols, step = plan.rows, plan.tile_cols, plan.step
    late, blocks = plan.late, plan.blocks
    here = lax.axis_index("gx")
    is_even = here % 2 == 0
    first_col = here * tile_cols
    fill_extended(plan, own, near, far, extended)
    first = jnp.where(is_even, 0, blocks - late)
    for index in range(late):
        fill_patches(plan, first + index, index, extended, turned, pairs_ref, patches)
    field[0 : late * rows, :] = lax.dot_general(
        patches[...], bands[...], NT, preferred_element_type=jnp.float32
    )

    def field_piece(block, t, start):
        slot = jnp.where(is_even, block, (block + late) % blocks)
        first = pl.multiple_of(slot * rows + start, 8)
        return field[pl.ds(first, CHUNK), t * LANES : (t + 1) * LANES]

    lane = lane_index(CHUNK, WIDE)
    near_lane = lane_index(CHUNK, LANES)
    col = lane + (first_col - plan.field_halo)
    inside = (col >= 0) & (col < plan.cols)
    kernels_count = plan.channels // 2
    for image in (intensity, develop, resid, dense_grad):
        image[0:PAD, :] = jnp.zeros((PAD, WIDE), jnp.float32)
        image[PAD + rows : 3 * PAD + rows, :] = jnp.zeros((2 * PAD, WIDE), jnp.float32)

    def find_intensity(start):
        halves = [jnp.zeros((CHUNK, LANES), jnp.float32)] * (WIDE // LANES)
        for block in range(blocks):
            power = None
            for t in range(plan.wide // LANES):
                piece = field_piece(block, t, start)
                power = piece * piece if power is None else power + piece * piece
            power = power + roll_lanes(power, 2 * SLOT)
            power = power + roll_lanes(power, SLOT)
            power = roll_lanes(power, block * step)
            for half in range(WIDE // LANES):
                low_lane = block * step - half * LANES
                if -step < low_lane < LANES:
                    here_too = (near_lane >= low_lane) & (near_lane < low_lane + step)
                    halves[half] = jnp.where(here_too, power, halves[half])
        total = jnp.concatenate(halves, axis=1) / kernels_count
        intensity[pl.ds(PAD + start, CHUNK), :] = jnp.where(inside, total, 0.0)

    def find_develop(start):
        dense = smooth_chunk(intensity, start)
        value = jnp.where(inside, jax.nn.sigmoid(SHARPNESS * (dense - THRESHOLD)), 0.0)
        develop[pl.ds(PAD + start, CHUNK), :] = value

    def find_resid(start):
        printed = develop[pl.ds(PAD + start, CHUNK), :]
        for down, right, gain in zip(downs, rights, load_gains):
            printed = printed - gain * shifted_chunk(develop, start, down, right)
        target = roll_lanes(join_columns(plan, own, near, far, 1, start), -plan.radius)
        row = lax.broadcasted_iota(jnp.int32, (CHUNK, WIDE), 0) + start
        weight = (1.0 + 2.0 * row.astype(jnp.float32) / rows) * (
            1.0 + 2.0 * col.astype(jnp.float32) / plan.cols
        )
        diff = printed - target
        weighted = weight * diff
        resid[pl.ds(PAD + start, CHUNK), :] = jnp.where(inside, 2.0 * weighted, 0.0)
        mine = (lane >= plan.field_halo) & (lane < plan.field_halo + tile_cols)
        part = jnp.where(mine, weighted * diff, 0.0)
        return jnp.sum(part.reshape(CHUNK // 8, 8, WIDE), axis=0)

    def find_dense_grad(start):
        slope = resid[pl.ds(PAD + start, CHUNK), :]
        for down, right, gain in zip(downs, rights, load_gains):
            slope = slope - gain * shifted_chunk(resid, start, -down, -right)
        value = develop[pl.ds(PAD + start, CHUNK), :]
        dense_grad[pl.ds(PAD + start, CHUNK), :] = slope * SHARPNESS * value * (1.0 - value)

    used = inside & (lane >= plan.lo) & (lane < plan.hi)
    narrow = near_lane < step

    def find_products(start):
        inten_grad = smooth_chunk(dense_grad, start) * (2.0 / kernels_count)
        inten_grad = jnp.where(used, inten_grad, 0.0)
        halves = [inten_grad[:, h * LANES : (h + 1) * LANES] for h in range(WIDE // LANES)]
        gains = {}
        for block in range(plan.pieces[0][0], plan.pieces[-1][0] + 1):
            half, begin = divmod(block * step, LANES)
            part = halves[half]
            if begin + step > LANES:
                part = jnp.where(near_lane >= begin, part, halves[half + 1])
            part = jnp.where(narrow, roll_lanes(part, -begin), 0.0)
            part = part + roll_lanes(part, SLOT)
            gains[block] = part + roll_lanes(part, 2 * SLOT)
        for operand in range(plan.operand_blocks):
            sources = [p[0] for p in plan.pieces if p[1] == operand]
            for t in range(plan.wide // LANES):
                value = None
                for block in sources:
                    piece = field_piece(block, t, start) * gains[block]
                    value = piece if value is None else value + piece
                products[
                    pl.ds(operand * rows + start, CHUNK), t * LANES : (t + 1) * LANES
                ] = value.astype(jnp.bfloat16)

    each_chunk(rows, find_intensity)
    each_chunk(rows, find_develop)
    loss = jnp.sum(each_chunk(rows, find_resid))
    each_chunk(rows, find_dense_grad)
    each_chunk(rows, find_products)

    acc_rows, group_lanes = plan.acc_rows, 2 * LANES
    low[...] = jnp.zeros_like(low)
    high[...] = jnp.zeros_like(high)

    def add_groups(index, count):
        lanes = pl.ds(pl.multiple_of(index * 2 * group_lanes, LANES), count * group_lanes)
        out = lax.dot_general(
            products[...], bands[:, lanes], NN, preferred_element_type=jnp.float32
        )
        for operand in range(plan.operand_blocks):
            held = pl.ds(pl.multiple_of(operand * acc_rows + index * 8, 8), rows)
            block = slice(operand * rows, (operand + 1) * rows)
            low[held, :] += out[block, :group_lanes]
            if count == 2:
                high[held, :] += out[block, group_lanes:]

    def both_groups(index, carry):
        add_groups(index, 2)
        return carry

    groups = plan.pairs // 2
    lax.fori_loop(0, groups // 2, both_groups, 0)
    if groups % 2:
        add_groups(groups // 2, 1)

    start_row = plan.radius - 1
    count = -(-(rows + 1) // 8) * 8
    lane = lane_index(count, LANES)
    total = [None, None]
    for operand in range(plan.operand_blocks):
        base = operand * acc_rows + start_row
        pair = None
        for out, tap in ((low, 0), (low, 2), (high, 4), (high, 6)):
            lanes = slice(LANES, 2 * LANES) if tap % 4 else slice(0, LANES)
            piece = out[base - tap : base - tap + count, lanes]
            pair = piece if pair is None else pair + piece
        for _, index, shift, lowest, highest in plan.pieces:
            if index != operand:
                continue
            keep = (lane >= lowest + shift) & (lane < highest + shift)
            for a in range(2):
                piece = jnp.where(keep, roll_lanes(pair, shift - a * WINDOW), 0.0)
                total[a] = piece if total[a] is None else total[a] + piece
    tall[...] = total[0]
    gradient = tall[1 : 1 + rows, :] + total[1][:rows]
    square = jnp.sum(gradient * gradient)
    tall[0:rows, :] = gradient
    start = pl.multiple_of(lax.axis_index("gy") * plan.tile_rows, 8)
    grad_out[...] = tall[pl.ds(start, plan.tile_rows), :]
    sums_out[0:4, :] = jnp.broadcast_to(loss, (4, LANES))
    sums_out[4:8, :] = jnp.broadcast_to(square, (4, LANES))


def update_kernel(plan, mask, grad, *refs):
    *sums, update, loss = refs
    total = sums[0][...]
    for other in sums[1:]:
        total = total + other[...]
    scale = jnp.sqrt(total[4:5, :] / (plan.rows * plan.cols) + 1e-06)
    update[...] = mask[...] - (grad[...] / scale)[:, : plan.tile_cols]
    loss[...] = total[0:1, 0:1]


def partner(here, step, count):
    if count & (count - 1) == 0:
        return jnp.bitwise_xor(here, step)
    return lax.rem(here + step, count)


def fetch(value, axis, step, count):
    if count & (count - 1) == 0:
        pairs = [(i, i ^ step) for i in range(count)]
    else:
        pairs = [((i + step) % count, i) for i in range(count)]
    return lax.ppermute(value, axis, pairs)


def swap_neighbours(value, axis, count, first):
    pairs = []
    for i in range(first, count - 1, 2):
        pairs += [(i, i + 1), (i + 1, i)]
    if first and count % 2 == 0:
        pairs += [(0, count - 1), (count - 1, 0)]
    return lax.ppermute(value, axis, pairs)


def sum_terms(value, axis, count):
    if count & (count - 1):
        return [lax.psum(value, axis)]
    terms, bit = [value], 1
    while bit < count:
        value = functools.reduce(jnp.add, terms)
        steps = (bit, 2 * bit, 3 * bit) if 1 < bit and 2 * bit < count else (bit,)
        terms = [value] + [fetch(value, axis, s, count) for s in steps]
        bit *= 4 if len(steps) == 3 else 2
    return terms


def body(mask, target, kernels, offsets, load_weights):
    tile_rows, tile_cols = mask.shape
    ny, nx = lax.axis_size("gy"), lax.axis_size("gx")
    channels, taps = kernels.shape[0], kernels.shape[1]
    plan = Plan(tile_rows, tile_cols, ny, nx, channels, taps)
    rows = plan.rows

    def in_vmem(value):
        return pltpu.with_memory_space_constraint(value, pltpu.VMEM)

    def cost(nanoseconds):
        return pl.CostEstimate(flops=nanoseconds * 1000000, bytes_accessed=0, transcendentals=0)

    def params(scratch):
        return pltpu.CompilerParams(vmem_limit_bytes=scratch + 12 * 1024 * 1024)

    both, mask = pl.pallas_call(
        functools.partial(pack_kernel, plan),
        out_shape=(
            pltpu.VMEM((2 * tile_rows, LANES), jnp.bfloat16),
            pltpu.VMEM((tile_rows, tile_cols), jnp.float32),
        ),
        in_specs=[pl.BlockSpec(memory_space=pltpu.HBM)] * 2,
        out_specs=(VMEM,) * 2,
        scratch_shapes=[
            pltpu.VMEM((tile_rows, tile_cols), jnp.int32),
            pltpu.SemaphoreType.DMA((2,)),
        ],
        compiler_params=params(0),
        name="pack",
    )(*[pltpu.with_memory_space_constraint(v, pltpu.HBM) for v in (mask, target)])
    pieces = [both] + [fetch(both, "gy", s, ny) for s in range(1, ny)]

    bands = pl.pallas_call(
        functools.partial(bands_kernel, plan),
        out_shape=pltpu.VMEM((plan.wide, plan.depth), jnp.bfloat16),
        in_specs=[VMEM],
        out_specs=VMEM,
        scratch_shapes=[
            pltpu.VMEM((2, channels, LANES), jnp.float32),
            pltpu.VMEM((plan.pairs * channels, LANES), jnp.float32),
        ],
        compiler_params=params(0),
        cost_estimate=cost(2000),
        name="bands",
    )(in_vmem(jnp.transpose(kernels, (1, 0, 2))))
    bands = in_vmem(bands)
    own, to_near, to_far = pl.pallas_call(
        functools.partial(strip_kernel, plan),
        out_shape=(
            pltpu.VMEM((2 * rows, LANES), jnp.bfloat16),
            pltpu.VMEM((rows, LANES), jnp.bfloat16),
            pltpu.VMEM((rows, LANES), jnp.bfloat16),
        ),
        in_specs=[VMEM] * ny + [pl.BlockSpec(memory_space=pl.ANY)],
        out_specs=(VMEM,) * 3,
        scratch_shapes=[pltpu.VMEM((2, rows, LANES), jnp.float32)],
        compiler_params=params(0),
        cost_estimate=cost(300),
        name="strip",
    )(*[in_vmem(p) for p in pieces], bands)
    near = in_vmem(swap_neighbours(to_near, "gx", nx, 0))
    far = in_vmem(swap_neighbours(to_far, "gx", nx, 1))
    own = in_vmem(own)

    tall_rows = TOP + rows + 32
    early = plan.blocks - plan.late
    patch_scratch = [
        pltpu.VMEM((tall_rows, WIDE), jnp.float32),
        pltpu.VMEM((tall_rows, LANES), jnp.float32),
        pltpu.VMEM((tall_rows, LANES), jnp.float32),
    ]
    field_type = pltpu.VMEM((plan.blocks * rows, plan.wide), jnp.float32)
    field = pl.pallas_call(
        functools.partial(early_kernel, plan),
        out_shape=field_type,
        in_specs=[VMEM] * 3,
        out_specs=VMEM,
        scratch_shapes=[
            *patch_scratch,
            pltpu.VMEM((early * rows, plan.depth), jnp.bfloat16),
        ],
        compiler_params=params(early * rows * plan.depth * 2),
        cost_estimate=cost(3500),
        name="early",
    )(own, near, bands)

    grad, sums, _ = pl.pallas_call(
        functools.partial(late_kernel, plan),
        out_shape=(
            pltpu.VMEM((tile_rows, LANES), jnp.float32),
            pltpu.VMEM((8, LANES), jnp.float32),
            field_type,
        ),
        in_specs=[VMEM] * 7,
        out_specs=(VMEM,) * 3,
        scratch_shapes=[
            *patch_scratch,
            pltpu.VMEM((plan.late * rows, plan.depth), jnp.bfloat16),
            *[pltpu.VMEM((rows + 3 * PAD, WIDE), jnp.float32)] * 4,
            pltpu.VMEM((plan.operand_blocks * rows, plan.wide), jnp.bfloat16),
            pltpu.VMEM((plan.operand_blocks * plan.acc_rows, 2 * LANES), jnp.float32),
            pltpu.VMEM((plan.operand_blocks * plan.acc_rows, 2 * LANES), jnp.float32),
            pltpu.VMEM((-(-(rows + 1) // 8) * 8, LANES), jnp.float32),
        ],
        input_output_aliases={6: 2},
        compiler_params=params(
            plan.late * rows * plan.depth * 2
            + plan.operand_blocks * (rows * plan.wide * 2 + plan.acc_rows * 16 * LANES)
        ),
        cost_estimate=cost(12000),
        name="late",
    )(in_vmem(jnp.transpose(offsets)), in_vmem(load_weights[None]), own, near, far, bands, in_vmem(field))

    terms = [in_vmem(t) for t in sum_terms(sums, "gx", nx)]
    update, loss = pl.pallas_call(
        functools.partial(update_kernel, plan),
        out_shape=(
            jax.ShapeDtypeStruct((tile_rows, tile_cols), jnp.float32),
            jax.ShapeDtypeStruct((1, 1), jnp.float32),
        ),
        in_specs=[VMEM] * (2 + len(terms)),
        out_specs=(VMEM, VMEM),
        compiler_params=params(0),
        name="update",
    )(in_vmem(mask), in_vmem(grad), *terms)
    return update, loss.reshape(())


def solution(mesh):
    return jax.shard_map(
        body,
        mesh=mesh,
        in_specs=(P("gy", "gx"), P("gy", "gx"), P(), P(), P()),
        out_specs=(P("gy", "gx"), P()),
        check_vma=False,
    )
```

```python
import functools

import jax
import jax.numpy as jnp
from jax import lax
from jax.experimental import pallas as pl
from jax.experimental.pallas import tpu as pltpu
from jax.sharding import PartitionSpec as P

REACH = 8
LOAD_TAPS = 8
SMOOTH = 2
SMOOTH_TAPS = (0.0625, 0.25, 0.375, 0.25, 0.0625)
SHARPNESS = 4.0
THRESHOLD = 0.65
LOADING_GAIN = 0.5

LANES = 128
WINDOW = 64
SLOT = 32
WIDE = 256
TOP = 24
CHUNK = 32
PAD = 8

NT = (((1,), (1,)), ((), ()))
NN = (((1,), (0,)), ((), ()))
VMEM = pl.BlockSpec(memory_space=pltpu.VMEM)


class Plan:
    def __init__(self, tile_rows, tile_cols, ny, nx, channels, taps):
        self.tile_rows, self.tile_cols, self.ny, self.nx = tile_rows, tile_cols, ny, nx
        self.rows, self.cols = tile_rows * ny, tile_cols * nx
        self.channels, self.taps, self.radius = channels, taps, taps // 2
        self.step = WINDOW - taps + 1
        self.field_halo = self.radius + 2 * (REACH + SMOOTH)
        self.halo = self.field_halo + self.radius
        self.blocks = -(-(tile_cols + 2 * self.field_halo) // self.step)
        self.pairs = -(-taps // 2)
        self.pairs += self.pairs % 2
        self.depth = self.pairs * LANES
        self.wide = channels * SLOT
        self.lo = self.field_halo - self.radius
        self.hi = self.field_halo + tile_cols + self.radius
        first, last = self.lo // self.step, (self.hi - 1) // self.step
        shift = self.field_halo + self.radius
        pieces = []
        for block in range(first, last + 1):
            low = max(0, shift - block * self.step)
            high = min(WINDOW, shift + tile_cols - block * self.step)
            pieces.append([block, block - first, block * self.step - shift, low, high])
        start = self.lo - first * self.step
        end = self.hi - last * self.step
        self.merged = (
            last > first
            and end <= start
            and end - 1 + taps - 1 < pieces[0][3]
            and start >= pieces[-1][4]
        )
        if self.merged:
            pieces[-1][1] = 0
        self.pieces = pieces
        self.operand_half = (max(p[1] for p in pieces) + 1) // 2
        self.operand_blocks = max(p[1] for p in pieces) + 1
        low = sum(b * self.step < self.halo for b in range(self.blocks))
        end = self.halo + tile_cols
        high = sum(b * self.step + WINDOW > end for b in range(self.blocks))
        self.late = max(low, high)
        self.acc_rows = -(-(self.rows + taps) // 8) * 8


def roll_lanes(value, shift):
    return pltpu.roll(value, shift % value.shape[1], 1)


def lane_index(rows, lanes):
    return lax.broadcasted_iota(jnp.int32, (rows, lanes), 1)


def shifted_chunk(ref, start, down, right):
    rest = lax.rem(PAD + down, 8)
    base = pl.multiple_of(start + PAD + down - rest, 8)
    tiles = ref[pl.ds(base, CHUNK + 8), :].reshape(CHUNK // 8 + 1, 8, WIDE)
    tiles = pltpu.roll(tiles, lax.rem(8 - rest, 8), 1)
    row = lax.broadcasted_iota(jnp.int32, (CHUNK // 8, 8, WIDE), 1)
    value = jnp.where(row < 8 - rest, tiles[:-1], tiles[1:]).reshape(CHUNK, WIDE)
    return pltpu.roll(value, lax.rem(WIDE - right, WIDE), 1)


def pack_kernel(plan, mask, target, both, mask_out, target_in, sems):
    rows, cols = plan.tile_rows, plan.tile_cols
    copies = [
        pltpu.make_async_copy(source, held, sems.at[i])
        for i, (source, held) in enumerate(((mask, mask_out), (target, target_in)))
    ]
    for copy in copies:
        copy.start()
    if cols < LANES:
        both[...] = jnp.zeros_like(both)
    copies[0].wait()
    both[0:rows, 0:cols] = mask_out[...].astype(jnp.bfloat16)
    copies[1].wait()
    both[rows : 2 * rows, 0:cols] = target_in[...].astype(jnp.float32).astype(jnp.bfloat16)


def entries(row):
    column = lane_index(1, row.shape[1])
    return [jnp.sum(jnp.where(column == i, row, 0)) for i in range(row.shape[1])]


def strip_kernel(plan, *refs):
    pieces, (out, to_near, to_far, hold) = refs[: plan.ny], refs[plan.ny + 1 :]
    here = lax.axis_index("gy")
    tile_rows, rows = plan.tile_rows, plan.rows
    for index, piece in enumerate(pieces):
        source = partner(here, index, plan.ny)
        value = piece[...].astype(jnp.float32)
        start = pl.multiple_of(source * tile_rows, 8)
        hold[0, pl.ds(start, tile_rows), :] = value[:tile_rows]
        hold[1, pl.ds(start, tile_rows), :] = value[tile_rows:]
    out[0:rows, :] = hold[0].astype(jnp.bfloat16)
    out[rows : 2 * rows, :] = hold[1].astype(jnp.bfloat16)
    even = lax.axis_index("gx") % 2 == 0
    cols = plan.tile_cols
    first = lane_index(rows, LANES) < WINDOW
    low = jnp.where(first, hold[0], roll_lanes(hold[1], WINDOW))
    high = jnp.where(first, roll_lanes(hold[0], WINDOW - cols), roll_lanes(hold[1], LANES - cols))
    to_near[...] = jnp.where(even, high, low).astype(jnp.bfloat16)
    to_far[...] = jnp.where(even, low, high).astype(jnp.bfloat16)


def bands_kernel(plan, kernels_ref, bands, row_ref, pairs_ref):
    channels, taps = plan.channels, plan.taps
    row_ref[...] = jnp.zeros_like(row_ref)
    for q in range(plan.pairs):
        for a in range(2):
            if 2 * q + a < taps:
                row_ref[a, :, 0:taps] = kernels_ref[2 * q + a].astype(jnp.float32)
            else:
                row_ref[a] = jnp.zeros((channels, LANES), jnp.float32)
        pairs_ref[q * channels : (q + 1) * channels, :] = row_ref[0] + roll_lanes(row_ref[1], WINDOW)

    def channel(c, _):
        for q in range(plan.pairs):
            row = pairs_ref[pl.ds(q * channels + c, 1), :]
            wide = jnp.broadcast_to(row, (SLOT, LANES))
            rolled = pltpu.roll(wide, 0, 1, stride=1, stride_axis=0)
            bands[pl.ds(pl.multiple_of(c * SLOT, SLOT), SLOT), q * LANES : (q + 1) * LANES] = (
                rolled.astype(jnp.bfloat16)
            )
        return 0

    lax.fori_loop(0, channels, channel, 0)


def smooth_chunk(ref, start):
    rows = [chunk_at(ref, start, PAD + a) for a in (-2, -1, 0, 1, 2)]
    total = SMOOTH_TAPS[2] * rows[2]
    total = total + SMOOTH_TAPS[1] * (rows[1] + rows[3]) + SMOOTH_TAPS[0] * (rows[0] + rows[4])
    cols = [total if b == 0 else roll_lanes(total, -b) for b in (-2, -1, 0, 1, 2)]
    total = SMOOTH_TAPS[2] * cols[2]
    return total + SMOOTH_TAPS[1] * (cols[1] + cols[3]) + SMOOTH_TAPS[0] * (cols[0] + cols[4])


def widen(value):
    return jnp.concatenate([value, jnp.zeros_like(value)], axis=1)


def each_chunk(rows, work):
    count = rows // CHUNK
    if count <= 24:
        results = [work(i * CHUNK) for i in range(count)]
        return None if results[0] is None else functools.reduce(jnp.add, results)
    zero = jax.eval_shape(lambda: work(0))

    def step(index, total):
        result = work(pl.multiple_of(index * CHUNK, CHUNK))
        return None if result is None else total + result

    return lax.fori_loop(0, count, step, None if zero is None else jnp.zeros(zero.shape, zero.dtype))


def chunk_at(ref, start, offset):
    if isinstance(start, int):
        return ref[start + offset : start + offset + CHUNK, :]
    return ref[pl.ds(start, CHUNK + 2 * PAD), :][offset : offset + CHUNK]


def join_columns(plan, own, near, far, part, start):
    tile_cols, halo = plan.tile_cols, plan.halo
    here = lax.axis_index("gx")
    even = here % 2 == 0
    lane = lane_index(CHUNK, WIDE)
    to_right = halo + tile_cols
    on_left, on_right = lane < halo, (lane >= to_right) & (lane < to_right + halo)

    def side(ref, right):
        shift = jnp.where(right, to_right, halo - WINDOW) + (WIDE - part * WINDOW)
        value = widen(ref[pl.ds(start, CHUNK), :].astype(jnp.float32))
        return pltpu.roll(value, shift % WIDE, 1), (on_left & ~right) | (on_right & right)

    mine = widen(own[pl.ds(part * plan.rows + start, CHUNK), :].astype(jnp.float32))
    value, there = side(near, even)
    joined = jnp.where(there, value, 0.0)
    joined = jnp.where((lane >= halo) & (lane < to_right), roll_lanes(mine, halo), joined)
    if far is not None:
        value, there = side(far, ~even)
        exists = jnp.where(even, here > 0, here < plan.nx - 1)
        joined = jnp.where(there & exists, value, joined)
    return joined


def fill_extended(plan, own, near, far, extended):
    rows, tall_rows = plan.rows, extended.shape[0]
    extended[0:TOP, :] = jnp.zeros((TOP, WIDE), jnp.float32)
    extended[TOP + rows : tall_rows, :] = jnp.zeros((tall_rows - TOP - rows, WIDE), jnp.float32)

    def fill(start):
        extended[pl.ds(TOP + start, CHUNK), :] = join_columns(plan, own, near, far, 0, start)

    each_chunk(rows, fill)


def fill_patches(plan, block, index, extended, turned, pairs_ref, patches):
    rows, body_rows = plan.rows, extended.shape[0] - 8
    half = lane_index(body_rows, LANES) < WINDOW
    window = pltpu.roll(extended[...], lax.rem(WIDE - block * plan.step, WIDE), 1)[:, :LANES]
    turned[...] = roll_lanes(window, WINDOW)
    pairs_ref[0:body_rows, :] = jnp.where(half, window[0:body_rows], turned[1 : body_rows + 1, :])
    for q in range(8):
        start = TOP - plan.radius + 2 * q
        uses = range(q, plan.pairs, 8)
        height = rows + 16 * (len(uses) - 1)
        value = pairs_ref[start : start + height, :].astype(jnp.bfloat16)
        for tile, pair in enumerate(uses):
            patches[index * rows : (index + 1) * rows, pair * LANES : (pair + 1) * LANES] = value[
                16 * tile : 16 * tile + rows
            ]


def find_field(plan, slot, count, patches, bands, field, power, meanwhile=()):
    rows = plan.rows
    first = slot * rows

    def add_squares(lanes, is_last):
        def add(start):
            held = pl.ds(first + start, CHUNK)
            total = None if lanes.start == 0 else power[held, :]
            for low in range(lanes.start, lanes.stop, LANES):
                piece = field[held, low : low + LANES]
                total = piece * piece if total is None else total + piece * piece
            if is_last:
                total = total + roll_lanes(total, 2 * SLOT)
                total = total + roll_lanes(total, SLOT)
            power[held, :] = total

        each_chunk(count * rows, add)

    last = None
    for low in range(0, plan.wide, 2 * LANES):
        lanes = slice(low, min(low + 2 * LANES, plan.wide))
        field[first : first + count * rows, lanes] = lax.dot_general(
            patches[...], bands[lanes, :], NT, preferred_element_type=jnp.float32
        )
        if last is not None:
            add_squares(last, False)
        if low == 2 * LANES:
            for work in meanwhile:
                work()
        last = lanes
    add_squares(last, True)


def early_kernel(
    plan, own, near, bands, field, power, extended, turned, pairs_ref, patches
):
    late, blocks = plan.late, plan.blocks
    fill_extended(plan, own, near, None, extended)
    first = jnp.where(lax.axis_index("gx") % 2 == 0, late, 0)
    for index in range(blocks - late):
        fill_patches(plan, first + index, index, extended, turned, pairs_ref, patches)
    find_field(plan, late, blocks - late, patches, bands, field, power)


def late_kernel(
    plan,
    offsets,
    load_weights,
    own,
    near,
    far,
    bands,
    field_in,
    power_in,
    grad_out,
    sums_out,
    field,
    power,
    extended,
    turned,
    pairs_ref,
    patches,
    intensity,
    develop,
    resid,
    dense_grad,
    inten_grad,
    target,
    products,
    products_two,
    low,
    high,
    tall,
):
    del field_in, power_in
    downs, rights = (entries(offsets[axis : axis + 1, :]) for axis in range(2))
    load_gains = entries(load_weights[...] * (LOADING_GAIN / LOAD_TAPS))
    rows, tile_cols, step = plan.rows, plan.tile_cols, plan.step
    late, blocks = plan.late, plan.blocks
    here = lax.axis_index("gx")
    is_even = here % 2 == 0
    first_col = here * tile_cols
    fill_extended(plan, own, near, far, extended)
    first = jnp.where(is_even, 0, blocks - late)
    for index in range(late):
        fill_patches(plan, first + index, index, extended, turned, pairs_ref, patches)

    def find_target(start):
        joined = join_columns(plan, own, near, far, 1, start)
        target[pl.ds(start, CHUNK), :] = roll_lanes(joined, -plan.radius)

    def clear():
        low[...] = jnp.zeros_like(low)
        high[...] = jnp.zeros_like(high)
        for image in (intensity, develop, resid, dense_grad):
            image[0:PAD, :] = jnp.zeros((PAD, WIDE), jnp.float32)
            image[PAD + rows : 3 * PAD + rows, :] = jnp.zeros((2 * PAD, WIDE), jnp.float32)

    meanwhile = (lambda: each_chunk(rows, find_target), clear)
    find_field(plan, 0, late, patches, bands, field, power, meanwhile)

    def slot_row(block, start):
        slot = jnp.where(is_even, block, (block + late) % blocks)
        return pl.multiple_of(slot * rows + start, 8)

    lane = lane_index(CHUNK, WIDE)
    near_lane = lane_index(CHUNK, LANES)
    col = lane + (first_col - plan.field_halo)
    inside = (col >= 0) & (col < plan.cols)
    kernels_count = plan.channels // 2

    def find_intensity(start):
        halves = [jnp.zeros((CHUNK, LANES), jnp.float32)] * (WIDE // LANES)
        for block in range(blocks):
            total = power[pl.ds(slot_row(block, start), CHUNK), :]
            total = roll_lanes(total, block * step)
            for half in range(WIDE // LANES):
                low_lane = block * step - half * LANES
                if -step < low_lane < LANES:
                    here_too = (near_lane >= low_lane) & (near_lane < low_lane + step)
                    halves[half] = jnp.where(here_too, total, halves[half])
        total = jnp.concatenate(halves, axis=1) / kernels_count
        intensity[pl.ds(PAD + start, CHUNK), :] = jnp.where(inside, total, 0.0)

    def find_develop(start):
        dense = smooth_chunk(intensity, start)
        value = jnp.where(inside, jax.nn.sigmoid(SHARPNESS * (dense - THRESHOLD)), 0.0)
        develop[pl.ds(PAD + start, CHUNK), :] = value

    def find_resid(start):
        printed = develop[pl.ds(PAD + start, CHUNK), :]
        for down, right, gain in zip(downs, rights, load_gains):
            printed = printed - gain * shifted_chunk(develop, start, down, right)
        row = lax.broadcasted_iota(jnp.int32, (CHUNK, WIDE), 0) + start
        weight = (1.0 + 2.0 * row.astype(jnp.float32) / rows) * (
            1.0 + 2.0 * col.astype(jnp.float32) / plan.cols
        )
        diff = printed - target[pl.ds(start, CHUNK), :]
        weighted = weight * diff
        resid[pl.ds(PAD + start, CHUNK), :] = jnp.where(inside, 2.0 * weighted, 0.0)
        mine = (lane >= plan.field_halo) & (lane < plan.field_halo + tile_cols)
        part = jnp.where(mine, weighted * diff, 0.0)
        return jnp.sum(part.reshape(CHUNK // 8, 8, WIDE), axis=0)

    def find_dense_grad(start):
        slope = resid[pl.ds(PAD + start, CHUNK), :]
        for down, right, gain in zip(downs, rights, load_gains):
            slope = slope - gain * shifted_chunk(resid, start, -down, -right)
        value = develop[pl.ds(PAD + start, CHUNK), :]
        dense_grad[pl.ds(PAD + start, CHUNK), :] = slope * SHARPNESS * value * (1.0 - value)

    used = inside & (lane >= plan.lo) & (lane < plan.hi)
    narrow = near_lane < step

    def find_inten_grad(start):
        value = smooth_chunk(dense_grad, start) * (2.0 / kernels_count)
        inten_grad[pl.ds(start, CHUNK), :] = jnp.where(used, value, 0.0)

    def find_products(operands, ref, start):
        wide = inten_grad[pl.ds(start, CHUNK), :]
        halves = [wide[:, h * LANES : (h + 1) * LANES] for h in range(WIDE // LANES)]
        for index, operand in enumerate(operands):
            sources = []
            for block in (p[0] for p in plan.pieces if p[1] == operand):
                half, begin = divmod(block * step, LANES)
                part = halves[half]
                if begin + step > LANES:
                    part = jnp.where(near_lane >= begin, part, halves[half + 1])
                part = jnp.where(narrow, roll_lanes(part, -begin), 0.0)
                part = part + roll_lanes(part, SLOT)
                sources.append((slot_row(block, start), part + roll_lanes(part, 2 * SLOT)))
            for t in range(plan.wide // LANES):
                lanes = slice(t * LANES, (t + 1) * LANES)
                terms = [field[pl.ds(first, CHUNK), lanes] * gain for first, gain in sources]
                ref[pl.ds(index * rows + start, CHUNK), lanes] = functools.reduce(
                    jnp.add, terms
                ).astype(jnp.bfloat16)

    acc_rows, group_lanes = plan.acc_rows, 2 * LANES
    groups = plan.pairs // 2

    def add_group(operands, ref, group):
        out = lax.dot_general(
            ref[...],
            bands[:, group * group_lanes : (group + 1) * group_lanes],
            NN,
            preferred_element_type=jnp.float32,
        )
        held = high if group % 2 else low
        for index, operand in enumerate(operands):
            first = operand * acc_rows + group // 2 * 8
            held[first : first + rows, :] += out[index * rows : (index + 1) * rows, :]

    each_chunk(rows, find_intensity)
    each_chunk(rows, find_develop)
    loss = jnp.sum(each_chunk(rows, find_resid))
    each_chunk(rows, find_dense_grad)
    each_chunk(rows, find_inten_grad)
    halves_of = [range(plan.operand_half), range(plan.operand_half, plan.operand_blocks)]
    each_chunk(rows, functools.partial(find_products, halves_of[0], products))
    chunks = rows // CHUNK
    if chunks > groups:
        each_chunk(rows, functools.partial(find_products, halves_of[1], products_two))
    for group in range(groups):
        add_group(halves_of[0], products, group)
        if group < chunks <= groups:
            find_products(halves_of[1], products_two, group * CHUNK)

    start_row = plan.radius - 1
    count = tall.shape[1]
    gather_lane = lane_index(count, LANES)

    def gather(operand):
        base = operand * acc_rows + start_row
        pair = None
        for out, tap in ((low, 0), (low, 2), (high, 4), (high, 6)):
            lanes = slice(LANES, 2 * LANES) if tap % 4 else slice(0, LANES)
            piece = out[base - tap : base - tap + count, lanes]
            pair = piece if pair is None else pair + piece
        for a in range(2):
            total = None if operand == 0 else tall[a]
            for _, index, shift, lowest, highest in plan.pieces:
                if index != operand:
                    continue
                keep = (gather_lane >= lowest + shift) & (gather_lane < highest + shift)
                piece = jnp.where(keep, roll_lanes(pair, shift - a * WINDOW), 0.0)
                total = piece if total is None else total + piece
            tall[a] = total

    for group in range(groups):
        add_group(halves_of[1], products_two, group)
        if group < len(halves_of[0]):
            gather(halves_of[0][group])
    for operand in [*halves_of[0][groups:], *halves_of[1]]:
        gather(operand)
    gradient = tall[0, 1 : 1 + rows, :] + tall[1, 0:rows, :]
    square = jnp.sum(gradient * gradient)
    tall[0, 0:rows, :] = gradient
    start = pl.multiple_of(lax.axis_index("gy") * plan.tile_rows, 8)
    grad_out[...] = tall[0, pl.ds(start, plan.tile_rows), :]
    sums_out[0:4, :] = jnp.broadcast_to(loss, (4, LANES))
    sums_out[4:8, :] = jnp.broadcast_to(square, (4, LANES))


def update_kernel(plan, mask, grad, *refs):
    *sums, update, loss = refs
    total = sums[0][...]
    for other in sums[1:]:
        total = total + other[...]
    scale = jnp.sqrt(total[4:5, :] / (plan.rows * plan.cols) + 1e-06)
    update[...] = mask[...] - (grad[...] / scale)[:, : plan.tile_cols]
    loss[...] = total[0:1, 0:1]


def partner(here, step, count):
    if count & (count - 1) == 0:
        return jnp.bitwise_xor(here, step)
    return lax.rem(here + step, count)


def fetch(value, axis, step, count):
    if count & (count - 1) == 0:
        pairs = [(i, i ^ step) for i in range(count)]
    else:
        pairs = [((i + step) % count, i) for i in range(count)]
    return lax.ppermute(value, axis, pairs)


def swap_neighbours(value, axis, count, first):
    pairs = []
    for i in range(first, count - 1, 2):
        pairs += [(i, i + 1), (i + 1, i)]
    if first and count % 2 == 0:
        pairs += [(0, count - 1), (count - 1, 0)]
    return lax.ppermute(value, axis, pairs)


def sum_terms(value, axis, count):
    if count & (count - 1):
        return [lax.psum(value, axis)]
    terms, bit = [value], 1
    while bit < count:
        value = functools.reduce(jnp.add, terms)
        steps = (bit, 2 * bit, 3 * bit) if 1 < bit and 2 * bit < count else (bit,)
        terms = [value] + [fetch(value, axis, s, count) for s in steps]
        bit *= 4 if len(steps) == 3 else 2
    return terms


def body(mask, target, kernels, offsets, load_weights):
    tile_rows, tile_cols = mask.shape
    ny, nx = lax.axis_size("gy"), lax.axis_size("gx")
    channels, taps = kernels.shape[0], kernels.shape[1]
    plan = Plan(tile_rows, tile_cols, ny, nx, channels, taps)
    rows = plan.rows

    def in_vmem(value):
        return pltpu.with_memory_space_constraint(value, pltpu.VMEM)

    def cost(nanoseconds):
        return pl.CostEstimate(flops=nanoseconds * 1000000, bytes_accessed=0, transcendentals=0)

    def params(scratch):
        return pltpu.CompilerParams(vmem_limit_bytes=scratch + 12 * 1024 * 1024)

    both, mask = pl.pallas_call(
        functools.partial(pack_kernel, plan),
        out_shape=(
            pltpu.VMEM((2 * tile_rows, LANES), jnp.bfloat16),
            pltpu.VMEM((tile_rows, tile_cols), jnp.float32),
        ),
        in_specs=[pl.BlockSpec(memory_space=pltpu.HBM)] * 2,
        out_specs=(VMEM,) * 2,
        scratch_shapes=[
            pltpu.VMEM((tile_rows, tile_cols), jnp.int32),
            pltpu.SemaphoreType.DMA((2,)),
        ],
        compiler_params=params(0),
        name="pack",
    )(*[pltpu.with_memory_space_constraint(v, pltpu.HBM) for v in (mask, target)])
    pieces = [both] + [fetch(both, "gy", s, ny) for s in range(1, ny)]

    bands = pl.pallas_call(
        functools.partial(bands_kernel, plan),
        out_shape=pltpu.VMEM((plan.wide, plan.depth), jnp.bfloat16),
        in_specs=[VMEM],
        out_specs=VMEM,
        scratch_shapes=[
            pltpu.VMEM((2, channels, LANES), jnp.float32),
            pltpu.VMEM((plan.pairs * channels, LANES), jnp.float32),
        ],
        compiler_params=params(0),
        cost_estimate=cost(2000),
        name="bands",
    )(in_vmem(jnp.transpose(kernels, (1, 0, 2))))
    bands = in_vmem(bands)
    own, to_near, to_far = pl.pallas_call(
        functools.partial(strip_kernel, plan),
        out_shape=(
            pltpu.VMEM((2 * rows, LANES), jnp.bfloat16),
            pltpu.VMEM((rows, LANES), jnp.bfloat16),
            pltpu.VMEM((rows, LANES), jnp.bfloat16),
        ),
        in_specs=[VMEM] * ny + [pl.BlockSpec(memory_space=pl.ANY)],
        out_specs=(VMEM,) * 3,
        scratch_shapes=[pltpu.VMEM((2, rows, LANES), jnp.float32)],
        compiler_params=params(0),
        cost_estimate=cost(300),
        name="strip",
    )(*[in_vmem(p) for p in pieces], bands)
    near = in_vmem(swap_neighbours(to_near, "gx", nx, 0))
    far = in_vmem(swap_neighbours(to_far, "gx", nx, 1))
    own = in_vmem(own)

    tall_rows = TOP + rows + 32
    early = plan.blocks - plan.late
    patch_scratch = [
        pltpu.VMEM((tall_rows, WIDE), jnp.float32),
        pltpu.VMEM((tall_rows, LANES), jnp.float32),
        pltpu.VMEM((tall_rows, LANES), jnp.float32),
    ]
    field_type = pltpu.VMEM((plan.blocks * rows, plan.wide), jnp.float32)
    power_type = pltpu.VMEM((plan.blocks * rows, LANES), jnp.float32)
    field, power = pl.pallas_call(
        functools.partial(early_kernel, plan),
        out_shape=(field_type, power_type),
        in_specs=[VMEM] * 3,
        out_specs=(VMEM,) * 2,
        scratch_shapes=[
            *patch_scratch,
            pltpu.VMEM((early * rows, plan.depth), jnp.bfloat16),
        ],
        compiler_params=params(early * rows * plan.depth * 2),
        cost_estimate=cost(3500),
        name="early",
    )(own, near, bands)

    grad, sums, _, _ = pl.pallas_call(
        functools.partial(late_kernel, plan),
        out_shape=(
            pltpu.VMEM((tile_rows, LANES), jnp.float32),
            pltpu.VMEM((8, LANES), jnp.float32),
            field_type,
            power_type,
        ),
        in_specs=[VMEM] * 8,
        out_specs=(VMEM,) * 4,
        scratch_shapes=[
            *patch_scratch,
            pltpu.VMEM((plan.late * rows, plan.depth), jnp.bfloat16),
            *[pltpu.VMEM((rows + 3 * PAD, WIDE), jnp.float32)] * 4,
            *[pltpu.VMEM((rows, WIDE), jnp.float32)] * 2,
            pltpu.VMEM((plan.operand_half * rows, plan.wide), jnp.bfloat16),
            pltpu.VMEM(((plan.operand_blocks - plan.operand_half) * rows, plan.wide), jnp.bfloat16),
            pltpu.VMEM((plan.operand_blocks * plan.acc_rows, 2 * LANES), jnp.float32),
            pltpu.VMEM((plan.operand_blocks * plan.acc_rows, 2 * LANES), jnp.float32),
            pltpu.VMEM((2, -(-(rows + 1) // 8) * 8, LANES), jnp.float32),
        ],
        input_output_aliases={6: 2, 7: 3},
        compiler_params=params(
            plan.late * rows * plan.depth * 2
            + plan.operand_blocks * (rows * plan.wide * 2 + plan.acc_rows * 16 * LANES)
        ),
        cost_estimate=cost(12000),
        name="late",
    )(in_vmem(jnp.transpose(offsets)), in_vmem(load_weights[None]), own, near, far, bands, in_vmem(field), in_vmem(power))

    terms = [in_vmem(t) for t in sum_terms(sums, "gx", nx)]
    update, loss = pl.pallas_call(
        functools.partial(update_kernel, plan),
        out_shape=(
            jax.ShapeDtypeStruct((tile_rows, tile_cols), jnp.float32),
            jax.ShapeDtypeStruct((1, 1), jnp.float32),
        ),
        in_specs=[VMEM] * (2 + len(terms)),
        out_specs=(VMEM, VMEM),
        compiler_params=params(0),
        name="update",
    )(in_vmem(mask), in_vmem(grad), *terms)
    return update, loss.reshape(())


def solution(mesh):
    return jax.shard_map(
        body,
        mesh=mesh,
        in_specs=(P("gy", "gx"), P("gy", "gx"), P(), P(), P()),
        out_specs=(P("gy", "gx"), P()),
        check_vma=False,
    )
```

```python
import functools

import jax
import jax.numpy as jnp
from jax import lax
from jax.experimental import pallas as pl
from jax.experimental.pallas import tpu as pltpu
from jax.sharding import PartitionSpec as P

REACH = 8
LOAD_TAPS = 8
SMOOTH = 2
SMOOTH_TAPS = (0.0625, 0.25, 0.375, 0.25, 0.0625)
SHARPNESS = 4.0
THRESHOLD = 0.65
LOADING_GAIN = 0.5

LANES = 128
WINDOW = 64
SLOT = 32
WIDE = 256
TOP = 24
CHUNK = 32
PAD = 8

NT = (((1,), (1,)), ((), ()))
NN = (((1,), (0,)), ((), ()))
VMEM = pl.BlockSpec(memory_space=pltpu.VMEM)


class Plan:
    def __init__(self, tile_rows, tile_cols, ny, nx, channels, taps):
        self.tile_rows, self.tile_cols, self.ny, self.nx = tile_rows, tile_cols, ny, nx
        self.rows, self.cols = tile_rows * ny, tile_cols * nx
        self.channels, self.taps, self.radius = channels, taps, taps // 2
        self.step = WINDOW - taps + 1
        self.field_halo = self.radius + 2 * (REACH + SMOOTH)
        self.halo = self.field_halo + self.radius
        self.blocks = -(-(tile_cols + 2 * self.field_halo) // self.step)
        self.pairs = -(-taps // 2)
        self.pairs += self.pairs % 2
        self.depth = self.pairs * LANES
        self.wide = channels * SLOT
        self.lo = self.field_halo - self.radius
        self.hi = self.field_halo + tile_cols + self.radius
        first, last = self.lo // self.step, (self.hi - 1) // self.step
        shift = self.field_halo + self.radius
        pieces = []
        for block in range(first, last + 1):
            low = max(0, shift - block * self.step)
            high = min(WINDOW, shift + tile_cols - block * self.step)
            pieces.append([block, block - first, block * self.step - shift, low, high])
        start = self.lo - first * self.step
        end = self.hi - last * self.step
        self.merged = (
            last > first
            and end <= start
            and end - 1 + taps - 1 < pieces[0][3]
            and start >= pieces[-1][4]
        )
        if self.merged:
            pieces[-1][1] = 0
        self.pieces = pieces
        self.operand_half = (max(p[1] for p in pieces) + 1) // 2
        self.operand_blocks = max(p[1] for p in pieces) + 1
        low = sum(b * self.step < self.halo for b in range(self.blocks))
        end = self.halo + tile_cols
        high = sum(b * self.step + WINDOW > end for b in range(self.blocks))
        self.late = max(low, high)
        self.acc_rows = -(-(self.rows + taps) // 8) * 8


def roll_lanes(value, shift):
    return pltpu.roll(value, shift % value.shape[1], 1)


def lane_index(rows, lanes):
    return lax.broadcasted_iota(jnp.int32, (rows, lanes), 1)


def shifted_chunk(ref, start, down, right):
    rest = lax.rem(PAD + down, 8)
    base = pl.multiple_of(start + PAD + down - rest, 8)
    tiles = ref[pl.ds(base, CHUNK + 8), :].reshape(CHUNK // 8 + 1, 8, WIDE)
    tiles = pltpu.roll(tiles, lax.rem(8 - rest, 8), 1)
    row = lax.broadcasted_iota(jnp.int32, (CHUNK // 8, 8, WIDE), 1)
    value = jnp.where(row < 8 - rest, tiles[:-1], tiles[1:]).reshape(CHUNK, WIDE)
    return pltpu.roll(value, lax.rem(WIDE - right, WIDE), 1)


def pack_kernel(plan, mask, target, both, mask_out, target_in, sems):
    rows, cols = plan.tile_rows, plan.tile_cols
    copies = [
        pltpu.make_async_copy(source, held, sems.at[i])
        for i, (source, held) in enumerate(((mask, mask_out), (target, target_in)))
    ]
    for copy in copies:
        copy.start()
    if cols < LANES:
        both[...] = jnp.zeros_like(both)
    copies[0].wait()
    both[0:rows, 0:cols] = mask_out[...].astype(jnp.bfloat16)
    copies[1].wait()
    both[rows : 2 * rows, 0:cols] = target_in[...].astype(jnp.float32).astype(jnp.bfloat16)


def entries(row):
    column = lane_index(1, row.shape[1])
    return [jnp.sum(jnp.where(column == i, row, 0)) for i in range(row.shape[1])]


def strip_kernel(plan, *refs):
    pieces, (out, to_near, to_far, hold) = refs[: plan.ny], refs[plan.ny + 1 :]
    here = lax.axis_index("gy")
    tile_rows, rows = plan.tile_rows, plan.rows
    for index, piece in enumerate(pieces):
        source = lax.rem(here + index, plan.ny)
        value = piece[...].astype(jnp.float32)
        start = pl.multiple_of(source * tile_rows, 8)
        hold[0, pl.ds(start, tile_rows), :] = value[:tile_rows]
        hold[1, pl.ds(start, tile_rows), :] = value[tile_rows:]
    out[0:rows, :] = hold[0].astype(jnp.bfloat16)
    out[rows : 2 * rows, :] = hold[1].astype(jnp.bfloat16)
    even = lax.axis_index("gx") % 2 == 0
    cols = plan.tile_cols
    first = lane_index(rows, LANES) < WINDOW
    low = jnp.where(first, hold[0], roll_lanes(hold[1], WINDOW))
    high = jnp.where(first, roll_lanes(hold[0], WINDOW - cols), roll_lanes(hold[1], LANES - cols))
    to_near[...] = jnp.where(even, high, low).astype(jnp.bfloat16)
    to_far[...] = jnp.where(even, low, high).astype(jnp.bfloat16)


def bands_kernel(plan, kernels_ref, bands, row_ref, pairs_ref):
    channels, taps = plan.channels, plan.taps
    row_ref[...] = jnp.zeros_like(row_ref)
    for q in range(plan.pairs):
        for a in range(2):
            if 2 * q + a < taps:
                row_ref[a, :, 0:taps] = kernels_ref[2 * q + a].astype(jnp.float32)
            else:
                row_ref[a] = jnp.zeros((channels, LANES), jnp.float32)
        pairs_ref[q * channels : (q + 1) * channels, :] = row_ref[0] + roll_lanes(row_ref[1], WINDOW)

    def channel(c, _):
        for q in range(plan.pairs):
            row = pairs_ref[pl.ds(q * channels + c, 1), :]
            wide = jnp.broadcast_to(row, (SLOT, LANES))
            rolled = pltpu.roll(wide, 0, 1, stride=1, stride_axis=0)
            bands[pl.ds(pl.multiple_of(c * SLOT, SLOT), SLOT), q * LANES : (q + 1) * LANES] = (
                rolled.astype(jnp.bfloat16)
            )
        return 0

    lax.fori_loop(0, channels, channel, 0, unroll=4)


def smooth_chunk(ref, start):
    rows = [chunk_at(ref, start, PAD + a) for a in (-2, -1, 0, 1, 2)]
    total = SMOOTH_TAPS[2] * rows[2]
    total = total + SMOOTH_TAPS[1] * (rows[1] + rows[3]) + SMOOTH_TAPS[0] * (rows[0] + rows[4])
    cols = [total if b == 0 else roll_lanes(total, -b) for b in (-2, -1, 0, 1, 2)]
    total = SMOOTH_TAPS[2] * cols[2]
    return total + SMOOTH_TAPS[1] * (cols[1] + cols[3]) + SMOOTH_TAPS[0] * (cols[0] + cols[4])


def widen(value):
    return jnp.concatenate([value, jnp.zeros_like(value)], axis=1)


def each_chunk(rows, work):
    count = rows // CHUNK
    if count <= 24:
        results = [work(i * CHUNK) for i in range(count)]
        return None if results[0] is None else functools.reduce(jnp.add, results)
    zero = jax.eval_shape(lambda: work(0))

    def step(index, total):
        result = work(pl.multiple_of(index * CHUNK, CHUNK))
        return None if result is None else total + result

    return lax.fori_loop(0, count, step, None if zero is None else jnp.zeros(zero.shape, zero.dtype))


def chunk_at(ref, start, offset):
    if isinstance(start, int):
        return ref[start + offset : start + offset + CHUNK, :]
    return ref[pl.ds(start, CHUNK + 2 * PAD), :][offset : offset + CHUNK]


def join_columns(plan, own, near, far, part, start):
    tile_cols, halo = plan.tile_cols, plan.halo
    here = lax.axis_index("gx")
    even = here % 2 == 0
    lane = lane_index(CHUNK, WIDE)
    to_right = halo + tile_cols
    on_left, on_right = lane < halo, (lane >= to_right) & (lane < to_right + halo)

    def side(ref, right):
        shift = jnp.where(right, to_right, halo - WINDOW) + (WIDE - part * WINDOW)
        value = widen(ref[pl.ds(start, CHUNK), :].astype(jnp.float32))
        return pltpu.roll(value, shift % WIDE, 1), (on_left & ~right) | (on_right & right)

    mine = widen(own[pl.ds(part * plan.rows + start, CHUNK), :].astype(jnp.float32))
    value, there = side(near, even)
    joined = jnp.where(there, value, 0.0)
    joined = jnp.where((lane >= halo) & (lane < to_right), roll_lanes(mine, halo), joined)
    if far is not None:
        value, there = side(far, ~even)
        exists = jnp.where(even, here > 0, here < plan.nx - 1)
        joined = jnp.where(there & exists, value, joined)
    return joined


def fill_extended(plan, own, near, far, extended):
    rows, tall_rows = plan.rows, extended.shape[0]
    extended[0:TOP, :] = jnp.zeros((TOP, WIDE), jnp.float32)
    extended[TOP + rows : tall_rows, :] = jnp.zeros((tall_rows - TOP - rows, WIDE), jnp.float32)

    def fill(start):
        extended[pl.ds(TOP + start, CHUNK), :] = join_columns(plan, own, near, far, 0, start)

    each_chunk(rows, fill)


def fill_patches(plan, block, index, extended, turned, pairs_ref, patches):
    rows, body_rows = plan.rows, extended.shape[0] - 8
    half = lane_index(body_rows, LANES) < WINDOW
    window = pltpu.roll(extended[...], lax.rem(WIDE - block * plan.step, WIDE), 1)[:, :LANES]
    turned[...] = roll_lanes(window, WINDOW)
    pairs_ref[0:body_rows, :] = jnp.where(half, window[0:body_rows], turned[1 : body_rows + 1, :])
    for q in range(8):
        start = TOP - plan.radius + 2 * q
        uses = range(q, plan.pairs, 8)
        height = rows + 16 * (len(uses) - 1)
        value = pairs_ref[start : start + height, :].astype(jnp.bfloat16)
        for tile, pair in enumerate(uses):
            patches[index * rows : (index + 1) * rows, pair * LANES : (pair + 1) * LANES] = value[
                16 * tile : 16 * tile + rows
            ]


def find_field(plan, slot, count, patches, bands, field, power, meanwhile=()):
    rows = plan.rows
    first = slot * rows

    def add_squares(lanes, is_last):
        def add(start):
            held = pl.ds(first + start, CHUNK)
            total = None if lanes.start == 0 else power[held, :]
            for low in range(lanes.start, lanes.stop, LANES):
                piece = field[held, low : low + LANES]
                total = piece * piece if total is None else total + piece * piece
            if is_last:
                total = total + roll_lanes(total, 2 * SLOT)
                total = total + roll_lanes(total, SLOT)
            power[held, :] = total

        each_chunk(count * rows, add)

    last = None
    for low in range(0, plan.wide, 2 * LANES):
        lanes = slice(low, min(low + 2 * LANES, plan.wide))
        field[first : first + count * rows, lanes] = lax.dot_general(
            patches[...], bands[lanes, :], NT, preferred_element_type=jnp.float32
        )
        if last is not None:
            add_squares(last, False)
        if low == 2 * LANES:
            for work in meanwhile:
                work()
        last = lanes
    add_squares(last, True)


def early_kernel(
    plan, own, near, bands, field, power, extended, turned, pairs_ref, patches
):
    late, blocks = plan.late, plan.blocks
    fill_extended(plan, own, near, None, extended)
    first = jnp.where(lax.axis_index("gx") % 2 == 0, late, 0)
    for index in range(blocks - late):
        fill_patches(plan, first + index, index, extended, turned, pairs_ref, patches)
    find_field(plan, late, blocks - late, patches, bands, field, power)


def late_kernel(
    plan,
    offsets,
    load_weights,
    own,
    near,
    far,
    bands,
    field_in,
    power_in,
    grad_out,
    sums_out,
    field,
    power,
    extended,
    turned,
    pairs_ref,
    patches,
    intensity,
    develop,
    resid,
    dense_grad,
    inten_grad,
    target,
    products,
    products_two,
    low,
    high,
    tall,
):
    del field_in, power_in
    downs, rights = (entries(offsets[axis : axis + 1, :]) for axis in range(2))
    load_gains = entries(load_weights[...] * (LOADING_GAIN / LOAD_TAPS))
    rows, tile_cols, step = plan.rows, plan.tile_cols, plan.step
    late, blocks = plan.late, plan.blocks
    here = lax.axis_index("gx")
    is_even = here % 2 == 0
    first_col = here * tile_cols
    fill_extended(plan, own, near, far, extended)
    first = jnp.where(is_even, 0, blocks - late)
    for index in range(late):
        fill_patches(plan, first + index, index, extended, turned, pairs_ref, patches)

    def find_target(start):
        joined = join_columns(plan, own, near, far, 1, start)
        target[pl.ds(start, CHUNK), :] = roll_lanes(joined, -plan.radius)

    def clear():
        low[...] = jnp.zeros_like(low)
        high[...] = jnp.zeros_like(high)
        for image in (intensity, develop, resid, dense_grad):
            image[0:PAD, :] = jnp.zeros((PAD, WIDE), jnp.float32)
            image[PAD + rows : 3 * PAD + rows, :] = jnp.zeros((2 * PAD, WIDE), jnp.float32)

    meanwhile = (lambda: each_chunk(rows, find_target), clear)
    find_field(plan, 0, late, patches, bands, field, power, meanwhile)

    def slot_row(block, start):
        slot = jnp.where(is_even, block, (block + late) % blocks)
        return pl.multiple_of(slot * rows + start, 8)

    lane = lane_index(CHUNK, WIDE)
    near_lane = lane_index(CHUNK, LANES)
    col = lane + (first_col - plan.field_halo)
    inside = (col >= 0) & (col < plan.cols)
    kernels_count = plan.channels // 2

    def find_intensity(start):
        halves = [jnp.zeros((CHUNK, LANES), jnp.float32)] * (WIDE // LANES)
        for block in range(blocks):
            total = power[pl.ds(slot_row(block, start), CHUNK), :]
            total = roll_lanes(total, block * step)
            for half in range(WIDE // LANES):
                low_lane = block * step - half * LANES
                if -step < low_lane < LANES:
                    here_too = (near_lane >= low_lane) & (near_lane < low_lane + step)
                    halves[half] = jnp.where(here_too, total, halves[half])
        total = jnp.concatenate(halves, axis=1) / kernels_count
        intensity[pl.ds(PAD + start, CHUNK), :] = jnp.where(inside, total, 0.0)

    def find_develop(start):
        dense = smooth_chunk(intensity, start)
        value = jnp.where(inside, jax.nn.sigmoid(SHARPNESS * (dense - THRESHOLD)), 0.0)
        develop[pl.ds(PAD + start, CHUNK), :] = value

    def find_resid(start):
        printed = develop[pl.ds(PAD + start, CHUNK), :]
        for down, right, gain in zip(downs, rights, load_gains):
            printed = printed - gain * shifted_chunk(develop, start, down, right)
        row = lax.broadcasted_iota(jnp.int32, (CHUNK, WIDE), 0) + start
        weight = (1.0 + 2.0 * row.astype(jnp.float32) / rows) * (
            1.0 + 2.0 * col.astype(jnp.float32) / plan.cols
        )
        diff = printed - target[pl.ds(start, CHUNK), :]
        weighted = weight * diff
        resid[pl.ds(PAD + start, CHUNK), :] = jnp.where(inside, 2.0 * weighted, 0.0)
        mine = (lane >= plan.field_halo) & (lane < plan.field_halo + tile_cols)
        part = jnp.where(mine, weighted * diff, 0.0)
        return jnp.sum(part.reshape(CHUNK // 8, 8, WIDE), axis=0)

    def find_dense_grad(start):
        slope = resid[pl.ds(PAD + start, CHUNK), :]
        for down, right, gain in zip(downs, rights, load_gains):
            slope = slope - gain * shifted_chunk(resid, start, -down, -right)
        value = develop[pl.ds(PAD + start, CHUNK), :]
        dense_grad[pl.ds(PAD + start, CHUNK), :] = slope * SHARPNESS * value * (1.0 - value)

    used = inside & (lane >= plan.lo) & (lane < plan.hi)
    narrow = near_lane < step

    def find_inten_grad(start):
        value = smooth_chunk(dense_grad, start) * (2.0 / kernels_count)
        inten_grad[pl.ds(start, CHUNK), :] = jnp.where(used, value, 0.0)

    def find_products(operands, ref, start):
        wide = inten_grad[pl.ds(start, CHUNK), :]
        halves = [wide[:, h * LANES : (h + 1) * LANES] for h in range(WIDE // LANES)]
        for index, operand in enumerate(operands):
            sources = []
            for block in (p[0] for p in plan.pieces if p[1] == operand):
                half, begin = divmod(block * step, LANES)
                part = halves[half]
                if begin + step > LANES:
                    part = jnp.where(near_lane >= begin, part, halves[half + 1])
                part = jnp.where(narrow, roll_lanes(part, -begin), 0.0)
                part = part + roll_lanes(part, SLOT)
                sources.append((slot_row(block, start), part + roll_lanes(part, 2 * SLOT)))
            for t in range(plan.wide // LANES):
                lanes = slice(t * LANES, (t + 1) * LANES)
                terms = [field[pl.ds(first, CHUNK), lanes] * gain for first, gain in sources]
                ref[pl.ds(index * rows + start, CHUNK), lanes] = functools.reduce(
                    jnp.add, terms
                ).astype(jnp.bfloat16)

    acc_rows, group_lanes = plan.acc_rows, 2 * LANES
    groups = plan.pairs // 2

    def add_group(operands, ref, group):
        out = lax.dot_general(
            ref[...],
            bands[:, group * group_lanes : (group + 1) * group_lanes],
            NN,
            preferred_element_type=jnp.float32,
        )
        held = high if group % 2 else low
        for index, operand in enumerate(operands):
            first = operand * acc_rows + group // 2 * 8
            held[first : first + rows, :] += out[index * rows : (index + 1) * rows, :]

    each_chunk(rows, find_intensity)
    each_chunk(rows, find_develop)
    loss = jnp.sum(each_chunk(rows, find_resid))
    each_chunk(rows, find_dense_grad)
    each_chunk(rows, find_inten_grad)
    halves_of = [range(plan.operand_half), range(plan.operand_half, plan.operand_blocks)]
    each_chunk(rows, functools.partial(find_products, halves_of[0], products))
    chunks = rows // CHUNK
    if chunks > groups:
        each_chunk(rows, functools.partial(find_products, halves_of[1], products_two))
    for group in range(groups):
        add_group(halves_of[0], products, group)
        if group < chunks <= groups:
            find_products(halves_of[1], products_two, group * CHUNK)

    start_row = plan.radius - 1
    count = tall.shape[1]
    gather_lane = lane_index(count, LANES)

    def gather(operand):
        base = operand * acc_rows + start_row
        pair = None
        for out, tap in ((low, 0), (low, 2), (high, 4), (high, 6)):
            lanes = slice(LANES, 2 * LANES) if tap % 4 else slice(0, LANES)
            piece = out[base - tap : base - tap + count, lanes]
            pair = piece if pair is None else pair + piece
        for a in range(2):
            total = None if operand == 0 else tall[a]
            for _, index, shift, lowest, highest in plan.pieces:
                if index != operand:
                    continue
                keep = (gather_lane >= lowest + shift) & (gather_lane < highest + shift)
                piece = jnp.where(keep, roll_lanes(pair, shift - a * WINDOW), 0.0)
                total = piece if total is None else total + piece
            tall[a] = total

    for group in range(groups):
        add_group(halves_of[1], products_two, group)
        if group < len(halves_of[0]):
            gather(halves_of[0][group])
    for operand in [*halves_of[0][groups:], *halves_of[1]]:
        gather(operand)
    gradient = tall[0, 1 : 1 + rows, :] + tall[1, 0:rows, :]
    square = jnp.sum(gradient * gradient)
    tall[0, 0:rows, :] = gradient
    start = pl.multiple_of(lax.axis_index("gy") * plan.tile_rows, 8)
    grad_out[...] = tall[0, pl.ds(start, plan.tile_rows), :]
    sums_out[0:4, :] = jnp.broadcast_to(loss, (4, LANES))
    sums_out[4:8, :] = jnp.broadcast_to(square, (4, LANES))


def update_kernel(plan, mask, grad, *refs):
    *sums, update, loss = refs
    total = sums[0][...]
    for other in sums[1:]:
        total = total + other[...]
    scale = jnp.sqrt(total[4:5, :] / (plan.rows * plan.cols) + 1e-06)
    update[...] = mask[...] - (grad[...] / scale)[:, : plan.tile_cols]
    loss[...] = total[0:1, 0:1]


def fetch(value, axis, step, count):
    if count & (count - 1) == 0:
        pairs = [(i, i ^ step) for i in range(count)]
    else:
        pairs = [((i + step) % count, i) for i in range(count)]
    return lax.ppermute(value, axis, pairs)


def swap_neighbours(value, axis, count, first):
    pairs = []
    for i in range(first, count - 1, 2):
        pairs += [(i, i + 1), (i + 1, i)]
    if first and count % 2 == 0:
        pairs += [(0, count - 1), (count - 1, 0)]
    return lax.ppermute(value, axis, pairs)


def sum_terms(value, axis, count):
    if count & (count - 1):
        return [lax.psum(value, axis)]
    terms, bit = [value], 1
    while bit < count:
        value = functools.reduce(jnp.add, terms)
        steps = (bit, 2 * bit, 3 * bit) if 1 < bit and 2 * bit < count else (bit,)
        terms = [value] + [fetch(value, axis, s, count) for s in steps]
        bit *= 4 if len(steps) == 3 else 2
    return terms


def body(mask, target, kernels, offsets, load_weights):
    tile_rows, tile_cols = mask.shape
    ny, nx = lax.axis_size("gy"), lax.axis_size("gx")
    channels, taps = kernels.shape[0], kernels.shape[1]
    plan = Plan(tile_rows, tile_cols, ny, nx, channels, taps)
    rows = plan.rows

    def in_vmem(value):
        return pltpu.with_memory_space_constraint(value, pltpu.VMEM)

    def cost(nanoseconds):
        return pl.CostEstimate(flops=nanoseconds * 1000000, bytes_accessed=0, transcendentals=0)

    def params(scratch):
        return pltpu.CompilerParams(vmem_limit_bytes=scratch + 12 * 1024 * 1024)

    both, mask = pl.pallas_call(
        functools.partial(pack_kernel, plan),
        out_shape=(
            pltpu.VMEM((2 * tile_rows, LANES), jnp.bfloat16),
            pltpu.VMEM((tile_rows, tile_cols), jnp.float32),
        ),
        in_specs=[pl.BlockSpec(memory_space=pltpu.HBM)] * 2,
        out_specs=(VMEM,) * 2,
        scratch_shapes=[
            pltpu.VMEM((tile_rows, tile_cols), jnp.int32),
            pltpu.SemaphoreType.DMA((2,)),
        ],
        compiler_params=params(0),
        name="pack",
    )(*[pltpu.with_memory_space_constraint(v, pltpu.HBM) for v in (mask, target)])
    pieces = [both] + [lax.ppermute(both, "gy", [((i + s) % ny, i) for i in range(ny)]) for s in range(1, ny)]

    bands = pl.pallas_call(
        functools.partial(bands_kernel, plan),
        out_shape=pltpu.VMEM((plan.wide, plan.depth), jnp.bfloat16),
        in_specs=[VMEM],
        out_specs=VMEM,
        scratch_shapes=[
            pltpu.VMEM((2, channels, LANES), jnp.float32),
            pltpu.VMEM((plan.pairs * channels, LANES), jnp.float32),
        ],
        compiler_params=params(0),
        cost_estimate=cost(2000),
        name="bands",
    )(in_vmem(jnp.transpose(kernels, (1, 0, 2))))
    bands = in_vmem(bands)
    own, to_near, to_far = pl.pallas_call(
        functools.partial(strip_kernel, plan),
        out_shape=(
            pltpu.VMEM((2 * rows, LANES), jnp.bfloat16),
            pltpu.VMEM((rows, LANES), jnp.bfloat16),
            pltpu.VMEM((rows, LANES), jnp.bfloat16),
        ),
        in_specs=[VMEM] * ny + [pl.BlockSpec(memory_space=pl.ANY)],
        out_specs=(VMEM,) * 3,
        scratch_shapes=[pltpu.VMEM((2, rows, LANES), jnp.float32)],
        compiler_params=params(0),
        cost_estimate=cost(300),
        name="strip",
    )(*[in_vmem(p) for p in pieces], bands)
    near = in_vmem(swap_neighbours(to_near, "gx", nx, 0))
    far = in_vmem(swap_neighbours(to_far, "gx", nx, 1))
    own = in_vmem(own)

    tall_rows = TOP + rows + 32
    early = plan.blocks - plan.late
    patch_scratch = [
        pltpu.VMEM((tall_rows, WIDE), jnp.float32),
        pltpu.VMEM((tall_rows, LANES), jnp.float32),
        pltpu.VMEM((tall_rows, LANES), jnp.float32),
    ]
    field_type = pltpu.VMEM((plan.blocks * rows, plan.wide), jnp.float32)
    power_type = pltpu.VMEM((plan.blocks * rows, LANES), jnp.float32)
    field, power = pl.pallas_call(
        functools.partial(early_kernel, plan),
        out_shape=(field_type, power_type),
        in_specs=[VMEM] * 3,
        out_specs=(VMEM,) * 2,
        scratch_shapes=[
            *patch_scratch,
            pltpu.VMEM((early * rows, plan.depth), jnp.bfloat16),
        ],
        compiler_params=params(early * rows * plan.depth * 2),
        cost_estimate=cost(3500),
        name="early",
    )(own, near, bands)

    grad, sums, _, _ = pl.pallas_call(
        functools.partial(late_kernel, plan),
        out_shape=(
            pltpu.VMEM((tile_rows, LANES), jnp.float32),
            pltpu.VMEM((8, LANES), jnp.float32),
            field_type,
            power_type,
        ),
        in_specs=[VMEM] * 8,
        out_specs=(VMEM,) * 4,
        scratch_shapes=[
            *patch_scratch,
            pltpu.VMEM((plan.late * rows, plan.depth), jnp.bfloat16),
            *[pltpu.VMEM((rows + 3 * PAD, WIDE), jnp.float32)] * 4,
            *[pltpu.VMEM((rows, WIDE), jnp.float32)] * 2,
            pltpu.VMEM((plan.operand_half * rows, plan.wide), jnp.bfloat16),
            pltpu.VMEM(((plan.operand_blocks - plan.operand_half) * rows, plan.wide), jnp.bfloat16),
            pltpu.VMEM((plan.operand_blocks * plan.acc_rows, 2 * LANES), jnp.float32),
            pltpu.VMEM((plan.operand_blocks * plan.acc_rows, 2 * LANES), jnp.float32),
            pltpu.VMEM((2, -(-(rows + 1) // 8) * 8, LANES), jnp.float32),
        ],
        input_output_aliases={6: 2, 7: 3},
        compiler_params=params(
            plan.late * rows * plan.depth * 2
            + plan.operand_blocks * (rows * plan.wide * 2 + plan.acc_rows * 16 * LANES)
        ),
        cost_estimate=cost(12000),
        name="late",
    )(in_vmem(jnp.transpose(offsets)), in_vmem(load_weights[None]), own, near, far, bands, in_vmem(field), in_vmem(power))

    terms = [in_vmem(t) for t in sum_terms(sums, "gx", nx)]
    update, loss = pl.pallas_call(
        functools.partial(update_kernel, plan),
        out_shape=(
            jax.ShapeDtypeStruct((tile_rows, tile_cols), jnp.float32),
            jax.ShapeDtypeStruct((1, 1), jnp.float32),
        ),
        in_specs=[VMEM] * (2 + len(terms)),
        out_specs=(VMEM, VMEM),
        compiler_params=params(0),
        name="update",
    )(in_vmem(mask), in_vmem(grad), *terms)
    return update, loss.reshape(())


def solution(mesh):
    return jax.shard_map(
        body,
        mesh=mesh,
        in_specs=(P("gy", "gx"), P("gy", "gx"), P(), P(), P()),
        out_specs=(P("gy", "gx"), P()),
        check_vma=False,
    )
```

```python
import functools

import jax
import jax.numpy as jnp
from jax import lax
from jax.experimental import pallas as pl
from jax.experimental.pallas import tpu as pltpu
from jax.sharding import PartitionSpec as P

REACH = 8
LOAD_TAPS = 8
SMOOTH = 2
SMOOTH_TAPS = (0.0625, 0.25, 0.375, 0.25, 0.0625)
SHARPNESS = 4.0
THRESHOLD = 0.65
LOADING_GAIN = 0.5

LANES = 128
WINDOW = 64
SLOT = 32
WIDE = 256
TOP = 24
CHUNK = 80
PAD = 8

NT = (((1,), (1,)), ((), ()))
NN = (((1,), (0,)), ((), ()))
VMEM = pl.BlockSpec(memory_space=pltpu.VMEM)


class Plan:
    def __init__(self, tile_rows, tile_cols, ny, nx, channels, taps):
        self.tile_rows, self.tile_cols, self.ny, self.nx = tile_rows, tile_cols, ny, nx
        self.rows, self.cols = tile_rows * ny, tile_cols * nx
        self.channels, self.taps, self.radius = channels, taps, taps // 2
        self.step = WINDOW - taps + 1
        self.field_halo = self.radius + 2 * (REACH + SMOOTH)
        self.halo = self.field_halo + self.radius
        self.blocks = -(-(tile_cols + 2 * self.field_halo) // self.step)
        self.pairs = -(-taps // 2)
        self.pairs += self.pairs % 2
        self.depth = self.pairs * LANES
        self.wide = channels * SLOT
        self.lo = self.field_halo - self.radius
        self.hi = self.field_halo + tile_cols + self.radius
        first, last = self.lo // self.step, (self.hi - 1) // self.step
        shift = self.field_halo + self.radius
        pieces = []
        for block in range(first, last + 1):
            low = max(0, shift - block * self.step)
            high = min(WINDOW, shift + tile_cols - block * self.step)
            pieces.append([block, block - first, block * self.step - shift, low, high])
        start = self.lo - first * self.step
        end = self.hi - last * self.step
        self.merged = (
            last > first
            and end <= start
            and end - 1 + taps - 1 < pieces[0][3]
            and start >= pieces[-1][4]
        )
        if self.merged:
            pieces[-1][1] = 0
        self.pieces = pieces
        self.operand_half = (max(p[1] for p in pieces) + 1) // 2
        self.operand_blocks = max(p[1] for p in pieces) + 1
        low = sum(b * self.step < self.halo for b in range(self.blocks))
        end = self.halo + tile_cols
        high = sum(b * self.step + WINDOW > end for b in range(self.blocks))
        self.late = max(low, high)
        self.acc_rows = -(-(self.rows + taps) // 8) * 8


def roll_lanes(value, shift):
    return pltpu.roll(value, shift % value.shape[1], 1)


def lane_index(rows, lanes):
    return lax.broadcasted_iota(jnp.int32, (rows, lanes), 1)


def shifted_chunk(ref, start, down, right):
    rest = lax.rem(PAD + down, 8)
    base = pl.multiple_of(start + PAD + down - rest, 8)
    tiles = ref[pl.ds(base, CHUNK + 8), :].reshape(CHUNK // 8 + 1, 8, WIDE)
    tiles = pltpu.roll(tiles, lax.rem(8 - rest, 8), 1)
    row = lax.broadcasted_iota(jnp.int32, (CHUNK // 8, 8, WIDE), 1)
    value = jnp.where(row < 8 - rest, tiles[:-1], tiles[1:]).reshape(CHUNK, WIDE)
    return pltpu.roll(value, lax.rem(WIDE - right, WIDE), 1)


def pack_kernel(plan, mask, target, both, mask_out, target_in, sems):
    rows, cols = plan.tile_rows, plan.tile_cols
    copies = [
        pltpu.make_async_copy(source, held, sems.at[i])
        for i, (source, held) in enumerate(((mask, mask_out), (target, target_in)))
    ]
    for copy in copies:
        copy.start()
    if cols < LANES:
        both[...] = jnp.zeros_like(both)
    copies[0].wait()
    both[0:rows, 0:cols] = mask_out[...].astype(jnp.bfloat16)
    copies[1].wait()
    both[rows : 2 * rows, 0:cols] = target_in[...].astype(jnp.float32).astype(jnp.bfloat16)


def entries(row):
    column = lane_index(1, row.shape[1])
    return [jnp.sum(jnp.where(column == i, row, 0)) for i in range(row.shape[1])]


def strip_kernel(plan, *refs):
    pieces, (out, to_near, to_far, hold) = refs[: plan.ny], refs[plan.ny + 1 :]
    here = lax.axis_index("gy")
    tile_rows, rows = plan.tile_rows, plan.rows
    for index, piece in enumerate(pieces):
        source = lax.rem(here + index, plan.ny)
        value = piece[...].astype(jnp.float32)
        start = pl.multiple_of(source * tile_rows, 8)
        hold[0, pl.ds(start, tile_rows), :] = value[:tile_rows]
        hold[1, pl.ds(start, tile_rows), :] = value[tile_rows:]
    out[0:rows, :] = hold[0].astype(jnp.bfloat16)
    out[rows : 2 * rows, :] = hold[1].astype(jnp.bfloat16)
    even = lax.axis_index("gx") % 2 == 0
    cols = plan.tile_cols
    first = lane_index(rows, LANES) < WINDOW
    low = jnp.where(first, hold[0], roll_lanes(hold[1], WINDOW))
    high = jnp.where(first, roll_lanes(hold[0], WINDOW - cols), roll_lanes(hold[1], LANES - cols))
    to_near[...] = jnp.where(even, high, low).astype(jnp.bfloat16)
    to_far[...] = jnp.where(even, low, high).astype(jnp.bfloat16)


def bands_kernel(plan, kernels_ref, bands, row_ref, pairs_ref):
    channels, taps = plan.channels, plan.taps
    row_ref[...] = jnp.zeros_like(row_ref)
    for q in range(plan.pairs):
        for a in range(2):
            if 2 * q + a < taps:
                row_ref[a, :, 0:taps] = kernels_ref[2 * q + a].astype(jnp.float32)
            else:
                row_ref[a] = jnp.zeros((channels, LANES), jnp.float32)
        pairs_ref[q * channels : (q + 1) * channels, :] = row_ref[0] + roll_lanes(row_ref[1], WINDOW)

    def channel(c, _):
        for q in range(plan.pairs):
            row = pairs_ref[pl.ds(q * channels + c, 1), :]
            wide = jnp.broadcast_to(row, (SLOT, LANES))
            rolled = pltpu.roll(wide, 0, 1, stride=1, stride_axis=0)
            bands[pl.ds(pl.multiple_of(c * SLOT, SLOT), SLOT), q * LANES : (q + 1) * LANES] = (
                rolled.astype(jnp.bfloat16)
            )
        return 0

    lax.fori_loop(0, channels, channel, 0, unroll=4)


def smooth_chunk(ref, start):
    rows = [chunk_at(ref, start, PAD + a) for a in (-2, -1, 0, 1, 2)]
    total = SMOOTH_TAPS[2] * rows[2]
    total = total + SMOOTH_TAPS[1] * (rows[1] + rows[3]) + SMOOTH_TAPS[0] * (rows[0] + rows[4])
    cols = [total if b == 0 else roll_lanes(total, -b) for b in (-2, -1, 0, 1, 2)]
    total = SMOOTH_TAPS[2] * cols[2]
    return total + SMOOTH_TAPS[1] * (cols[1] + cols[3]) + SMOOTH_TAPS[0] * (cols[0] + cols[4])


def widen(value):
    return jnp.concatenate([value, jnp.zeros_like(value)], axis=1)


def each_chunk(rows, work):
    count = rows // CHUNK
    if count <= 24:
        results = [work(i * CHUNK) for i in range(count)]
        return None if results[0] is None else functools.reduce(jnp.add, results)
    zero = jax.eval_shape(lambda: work(0))

    def step(index, total):
        result = work(pl.multiple_of(index * CHUNK, CHUNK))
        return None if result is None else total + result

    return lax.fori_loop(0, count, step, None if zero is None else jnp.zeros(zero.shape, zero.dtype))


def chunk_at(ref, start, offset):
    if isinstance(start, int):
        return ref[start + offset : start + offset + CHUNK, :]
    return ref[pl.ds(start, CHUNK + 2 * PAD), :][offset : offset + CHUNK]


def join_columns(plan, own, near, far, part, start):
    tile_cols, halo = plan.tile_cols, plan.halo
    here = lax.axis_index("gx")
    even = here % 2 == 0
    lane = lane_index(CHUNK, WIDE)
    to_right = halo + tile_cols
    on_left, on_right = lane < halo, (lane >= to_right) & (lane < to_right + halo)

    def side(ref, right):
        shift = jnp.where(right, to_right, halo - WINDOW) + (WIDE - part * WINDOW)
        value = widen(ref[pl.ds(start, CHUNK), :].astype(jnp.float32))
        return pltpu.roll(value, shift % WIDE, 1), (on_left & ~right) | (on_right & right)

    mine = widen(own[pl.ds(part * plan.rows + start, CHUNK), :].astype(jnp.float32))
    value, there = side(near, even)
    joined = jnp.where(there, value, 0.0)
    joined = jnp.where((lane >= halo) & (lane < to_right), roll_lanes(mine, halo), joined)
    if far is not None:
        value, there = side(far, ~even)
        exists = jnp.where(even, here > 0, here < plan.nx - 1)
        joined = jnp.where(there & exists, value, joined)
    return joined


def fill_extended(plan, own, near, far, extended):
    rows, tall_rows = plan.rows, extended.shape[0]
    extended[0:TOP, :] = jnp.zeros((TOP, WIDE), jnp.float32)
    extended[TOP + rows : tall_rows, :] = jnp.zeros((tall_rows - TOP - rows, WIDE), jnp.float32)

    def fill(start):
        extended[pl.ds(TOP + start, CHUNK), :] = join_columns(plan, own, near, far, 0, start)

    each_chunk(rows, fill)


def fill_patches(plan, block, index, extended, turned, pairs_ref, patches):
    rows, body_rows = plan.rows, extended.shape[0] - 8
    half = lane_index(body_rows, LANES) < WINDOW
    window = pltpu.roll(extended[...], lax.rem(WIDE - block * plan.step, WIDE), 1)[:, :LANES]
    turned[...] = roll_lanes(window, WINDOW)
    pairs_ref[0:body_rows, :] = jnp.where(half, window[0:body_rows], turned[1 : body_rows + 1, :])
    for q in range(8):
        start = TOP - plan.radius + 2 * q
        uses = range(q, plan.pairs, 8)
        height = rows + 16 * (len(uses) - 1)
        value = pairs_ref[start : start + height, :].astype(jnp.bfloat16)
        for tile, pair in enumerate(uses):
            patches[index * rows : (index + 1) * rows, pair * LANES : (pair + 1) * LANES] = value[
                16 * tile : 16 * tile + rows
            ]


def find_field(plan, slot, count, patches, bands, field, power, meanwhile=()):
    rows = plan.rows
    first = slot * rows

    def add_squares(lanes, is_last):
        def add(start):
            held = pl.ds(first + start, CHUNK)
            total = None if lanes.start == 0 else power[held, :]
            for low in range(lanes.start, lanes.stop, LANES):
                piece = field[held, low : low + LANES]
                total = piece * piece if total is None else total + piece * piece
            if is_last:
                total = total + roll_lanes(total, 2 * SLOT)
                total = total + roll_lanes(total, SLOT)
            power[held, :] = total

        each_chunk(count * rows, add)

    last = None
    for low in range(0, plan.wide, 2 * LANES):
        lanes = slice(low, min(low + 2 * LANES, plan.wide))
        field[first : first + count * rows, lanes] = lax.dot_general(
            patches[...], bands[lanes, :], NT, preferred_element_type=jnp.float32
        )
        if last is not None:
            add_squares(last, False)
        if low == 2 * LANES:
            for work in meanwhile:
                work()
        last = lanes
    add_squares(last, True)


def early_kernel(
    plan, own, near, bands, field, power, extended, turned, pairs_ref, patches
):
    late, blocks = plan.late, plan.blocks
    fill_extended(plan, own, near, None, extended)
    first = jnp.where(lax.axis_index("gx") % 2 == 0, late, 0)
    for index in range(blocks - late):
        fill_patches(plan, first + index, index, extended, turned, pairs_ref, patches)
    find_field(plan, late, blocks - late, patches, bands, field, power)


def late_kernel(
    plan,
    offsets,
    load_weights,
    own,
    near,
    far,
    bands,
    field_in,
    power_in,
    grad_out,
    sums_out,
    field,
    power,
    extended,
    turned,
    pairs_ref,
    patches,
    intensity,
    develop,
    resid,
    dense_grad,
    inten_grad,
    target,
    products,
    products_two,
    low,
    high,
    tall,
):
    del field_in, power_in
    downs, rights = (entries(offsets[axis : axis + 1, :]) for axis in range(2))
    load_gains = entries(load_weights[...] * (LOADING_GAIN / LOAD_TAPS))
    rows, tile_cols, step = plan.rows, plan.tile_cols, plan.step
    late, blocks = plan.late, plan.blocks
    here = lax.axis_index("gx")
    is_even = here % 2 == 0
    first_col = here * tile_cols
    fill_extended(plan, own, near, far, extended)
    first = jnp.where(is_even, 0, blocks - late)
    for index in range(late):
        fill_patches(plan, first + index, index, extended, turned, pairs_ref, patches)

    def find_target(start):
        joined = join_columns(plan, own, near, far, 1, start)
        target[pl.ds(start, CHUNK), :] = roll_lanes(joined, -plan.radius)

    def clear():
        low[...] = jnp.zeros_like(low)
        high[...] = jnp.zeros_like(high)
        for image in (intensity, develop, resid, dense_grad):
            image[0:PAD, :] = jnp.zeros((PAD, WIDE), jnp.float32)
            image[PAD + rows : 3 * PAD + rows, :] = jnp.zeros((2 * PAD, WIDE), jnp.float32)

    meanwhile = (lambda: each_chunk(rows, find_target), clear)
    find_field(plan, 0, late, patches, bands, field, power, meanwhile)

    def slot_row(block, start):
        slot = jnp.where(is_even, block, (block + late) % blocks)
        return pl.multiple_of(slot * rows + start, 8)

    lane = lane_index(CHUNK, WIDE)
    near_lane = lane_index(CHUNK, LANES)
    col = lane + (first_col - plan.field_halo)
    inside = (col >= 0) & (col < plan.cols)
    kernels_count = plan.channels // 2

    def find_intensity(start):
        halves = [jnp.zeros((CHUNK, LANES), jnp.float32)] * (WIDE // LANES)
        for block in range(blocks):
            total = power[pl.ds(slot_row(block, start), CHUNK), :]
            total = roll_lanes(total, block * step)
            for half in range(WIDE // LANES):
                low_lane = block * step - half * LANES
                if -step < low_lane < LANES:
                    here_too = (near_lane >= low_lane) & (near_lane < low_lane + step)
                    halves[half] = jnp.where(here_too, total, halves[half])
        total = jnp.concatenate(halves, axis=1) / kernels_count
        intensity[pl.ds(PAD + start, CHUNK), :] = jnp.where(inside, total, 0.0)

    def find_develop(start):
        dense = smooth_chunk(intensity, start)
        value = jnp.where(inside, jax.nn.sigmoid(SHARPNESS * (dense - THRESHOLD)), 0.0)
        develop[pl.ds(PAD + start, CHUNK), :] = value

    def find_resid(start):
        printed = develop[pl.ds(PAD + start, CHUNK), :]
        for down, right, gain in zip(downs, rights, load_gains):
            printed = printed - gain * shifted_chunk(develop, start, down, right)
        row = lax.broadcasted_iota(jnp.int32, (CHUNK, WIDE), 0) + start
        weight = (1.0 + 2.0 * row.astype(jnp.float32) / rows) * (
            1.0 + 2.0 * col.astype(jnp.float32) / plan.cols
        )
        diff = printed - target[pl.ds(start, CHUNK), :]
        weighted = weight * diff
        resid[pl.ds(PAD + start, CHUNK), :] = jnp.where(inside, 2.0 * weighted, 0.0)
        mine = (lane >= plan.field_halo) & (lane < plan.field_halo + tile_cols)
        part = jnp.where(mine, weighted * diff, 0.0)
        return jnp.sum(part.reshape(CHUNK // 8, 8, WIDE), axis=0)

    def find_dense_grad(start):
        slope = resid[pl.ds(PAD + start, CHUNK), :]
        for down, right, gain in zip(downs, rights, load_gains):
            slope = slope - gain * shifted_chunk(resid, start, -down, -right)
        value = develop[pl.ds(PAD + start, CHUNK), :]
        dense_grad[pl.ds(PAD + start, CHUNK), :] = slope * SHARPNESS * value * (1.0 - value)

    used = inside & (lane >= plan.lo) & (lane < plan.hi)
    narrow = near_lane < step

    def find_inten_grad(start):
        value = smooth_chunk(dense_grad, start) * (2.0 / kernels_count)
        inten_grad[pl.ds(start, CHUNK), :] = jnp.where(used, value, 0.0)

    def find_products(operands, ref, start):
        wide = inten_grad[pl.ds(start, CHUNK), :]
        halves = [wide[:, h * LANES : (h + 1) * LANES] for h in range(WIDE // LANES)]
        for index, operand in enumerate(operands):
            sources = []
            for block in (p[0] for p in plan.pieces if p[1] == operand):
                half, begin = divmod(block * step, LANES)
                part = halves[half]
                if begin + step > LANES:
                    part = jnp.where(near_lane >= begin, part, halves[half + 1])
                part = jnp.where(narrow, roll_lanes(part, -begin), 0.0)
                part = part + roll_lanes(part, SLOT)
                sources.append((slot_row(block, start), part + roll_lanes(part, 2 * SLOT)))
            for t in range(plan.wide // LANES):
                lanes = slice(t * LANES, (t + 1) * LANES)
                terms = [field[pl.ds(first, CHUNK), lanes] * gain for first, gain in sources]
                ref[pl.ds(index * rows + start, CHUNK), lanes] = functools.reduce(
                    jnp.add, terms
                ).astype(jnp.bfloat16)

    acc_rows, group_lanes = plan.acc_rows, 2 * LANES
    groups = plan.pairs // 2

    def add_group(operands, ref, group):
        out = lax.dot_general(
            ref[...],
            bands[:, group * group_lanes : (group + 1) * group_lanes],
            NN,
            preferred_element_type=jnp.float32,
        )
        held = high if group % 2 else low
        for index, operand in enumerate(operands):
            first = operand * acc_rows + group // 2 * 8
            held[first : first + rows, :] += out[index * rows : (index + 1) * rows, :]

    each_chunk(rows, find_intensity)
    each_chunk(rows, find_develop)
    loss = jnp.sum(each_chunk(rows, find_resid))
    each_chunk(rows, find_dense_grad)
    each_chunk(rows, find_inten_grad)
    halves_of = [range(plan.operand_half), range(plan.operand_half, plan.operand_blocks)]
    each_chunk(rows, functools.partial(find_products, halves_of[0], products))
    chunks = rows // CHUNK
    if chunks > groups:
        each_chunk(rows, functools.partial(find_products, halves_of[1], products_two))
    for group in range(groups):
        add_group(halves_of[0], products, group)
        if group < chunks <= groups:
            find_products(halves_of[1], products_two, group * CHUNK)

    start_row = plan.radius - 1
    count = tall.shape[1]
    gather_lane = lane_index(count, LANES)

    def gather(operand):
        base = operand * acc_rows + start_row
        pair = None
        for out, tap in ((low, 0), (low, 2), (high, 4), (high, 6)):
            lanes = slice(LANES, 2 * LANES) if tap % 4 else slice(0, LANES)
            piece = out[base - tap : base - tap + count, lanes]
            pair = piece if pair is None else pair + piece
        for a in range(2):
            total = None if operand == 0 else tall[a]
            for _, index, shift, lowest, highest in plan.pieces:
                if index != operand:
                    continue
                keep = (gather_lane >= lowest + shift) & (gather_lane < highest + shift)
                piece = jnp.where(keep, roll_lanes(pair, shift - a * WINDOW), 0.0)
                total = piece if total is None else total + piece
            tall[a] = total

    for group in range(groups):
        add_group(halves_of[1], products_two, group)
        if group < len(halves_of[0]):
            gather(halves_of[0][group])
    for operand in [*halves_of[0][groups:], *halves_of[1]]:
        gather(operand)
    gradient = tall[0, 1 : 1 + rows, :] + tall[1, 0:rows, :]
    square = jnp.sum(gradient * gradient)
    tall[0, 0:rows, :] = gradient
    start = pl.multiple_of(lax.axis_index("gy") * plan.tile_rows, 8)
    grad_out[...] = tall[0, pl.ds(start, plan.tile_rows), :]
    sums_out[0:4, :] = jnp.broadcast_to(loss, (4, LANES))
    sums_out[4:8, :] = jnp.broadcast_to(square, (4, LANES))


def update_kernel(plan, mask, grad, *refs):
    *sums, update, loss = refs
    total = sums[0][...]
    for other in sums[1:]:
        total = total + other[...]
    scale = jnp.sqrt(total[4:5, :] / (plan.rows * plan.cols) + 1e-06)
    update[...] = mask[...] - (grad[...] / scale)[:, : plan.tile_cols]
    loss[...] = total[0:1, 0:1]


def fetch(value, axis, step, count):
    if count & (count - 1) == 0:
        pairs = [(i, i ^ step) for i in range(count)]
    else:
        pairs = [((i + step) % count, i) for i in range(count)]
    return lax.ppermute(value, axis, pairs)


def swap_neighbours(value, axis, count, first):
    pairs = []
    for i in range(first, count - 1, 2):
        pairs += [(i, i + 1), (i + 1, i)]
    if first and count % 2 == 0:
        pairs += [(0, count - 1), (count - 1, 0)]
    return lax.ppermute(value, axis, pairs)


def sum_terms(value, axis, count):
    if count & (count - 1):
        return [lax.psum(value, axis)]
    terms, bit = [value], 1
    while bit < count:
        value = functools.reduce(jnp.add, terms)
        steps = (bit, 2 * bit, 3 * bit) if 1 < bit and 2 * bit < count else (bit,)
        if len(steps) == 3:
            terms = [value]
            for s in range(1, 4):
                pairs = [(i // (4 * bit) * 4 * bit + (i + s * bit) % (4 * bit), i) for i in range(count)]
                terms.append(lax.ppermute(value, axis, pairs))
        else:
            terms = [value] + [fetch(value, axis, s, count) for s in steps]
        bit *= 4 if len(steps) == 3 else 2
    return terms


def body(mask, target, kernels, offsets, load_weights):
    tile_rows, tile_cols = mask.shape
    ny, nx = lax.axis_size("gy"), lax.axis_size("gx")
    channels, taps = kernels.shape[0], kernels.shape[1]
    plan = Plan(tile_rows, tile_cols, ny, nx, channels, taps)
    rows = plan.rows

    def in_vmem(value):
        return pltpu.with_memory_space_constraint(value, pltpu.VMEM)

    def cost(nanoseconds):
        return pl.CostEstimate(flops=nanoseconds * 1000000, bytes_accessed=0, transcendentals=0)

    def params(scratch):
        return pltpu.CompilerParams(vmem_limit_bytes=scratch + 12 * 1024 * 1024)

    both, mask = pl.pallas_call(
        functools.partial(pack_kernel, plan),
        out_shape=(
            pltpu.VMEM((2 * tile_rows, LANES), jnp.bfloat16),
            pltpu.VMEM((tile_rows, tile_cols), jnp.float32),
        ),
        in_specs=[pl.BlockSpec(memory_space=pltpu.HBM)] * 2,
        out_specs=(VMEM,) * 2,
        scratch_shapes=[
            pltpu.VMEM((tile_rows, tile_cols), jnp.int32),
            pltpu.SemaphoreType.DMA((2,)),
        ],
        compiler_params=params(0),
        name="pack",
    )(*[pltpu.with_memory_space_constraint(v, pltpu.HBM) for v in (mask, target)])
    pieces = [both] + [lax.ppermute(both, "gy", [((i + s) % ny, i) for i in range(ny)]) for s in range(1, ny)]

    bands = pl.pallas_call(
        functools.partial(bands_kernel, plan),
        out_shape=pltpu.VMEM((plan.wide, plan.depth), jnp.bfloat16),
        in_specs=[VMEM],
        out_specs=VMEM,
        scratch_shapes=[
            pltpu.VMEM((2, channels, LANES), jnp.float32),
            pltpu.VMEM((plan.pairs * channels, LANES), jnp.float32),
        ],
        compiler_params=params(0),
        cost_estimate=cost(2000),
        name="bands",
    )(in_vmem(jnp.transpose(kernels, (1, 0, 2))))
    bands = in_vmem(bands)
    own, to_near, to_far = pl.pallas_call(
        functools.partial(strip_kernel, plan),
        out_shape=(
            pltpu.VMEM((2 * rows, LANES), jnp.bfloat16),
            pltpu.VMEM((rows, LANES), jnp.bfloat16),
            pltpu.VMEM((rows, LANES), jnp.bfloat16),
        ),
        in_specs=[VMEM] * ny + [pl.BlockSpec(memory_space=pl.ANY)],
        out_specs=(VMEM,) * 3,
        scratch_shapes=[pltpu.VMEM((2, rows, LANES), jnp.float32)],
        compiler_params=params(0),
        cost_estimate=cost(300),
        name="strip",
    )(*[in_vmem(p) for p in pieces], bands)
    near = in_vmem(swap_neighbours(to_near, "gx", nx, 0))
    far = in_vmem(swap_neighbours(to_far, "gx", nx, 1))
    own = in_vmem(own)

    tall_rows = TOP + rows + 32
    early = plan.blocks - plan.late
    patch_scratch = [
        pltpu.VMEM((tall_rows, WIDE), jnp.float32),
        pltpu.VMEM((tall_rows, LANES), jnp.float32),
        pltpu.VMEM((tall_rows, LANES), jnp.float32),
    ]
    field_type = pltpu.VMEM((plan.blocks * rows, plan.wide), jnp.float32)
    power_type = pltpu.VMEM((plan.blocks * rows, LANES), jnp.float32)
    field, power = pl.pallas_call(
        functools.partial(early_kernel, plan),
        out_shape=(field_type, power_type),
        in_specs=[VMEM] * 3,
        out_specs=(VMEM,) * 2,
        scratch_shapes=[
            *patch_scratch,
            pltpu.VMEM((early * rows, plan.depth), jnp.bfloat16),
        ],
        compiler_params=params(early * rows * plan.depth * 2),
        cost_estimate=cost(3500),
        name="early",
    )(own, near, bands)

    grad, sums, _, _ = pl.pallas_call(
        functools.partial(late_kernel, plan),
        out_shape=(
            pltpu.VMEM((tile_rows, LANES), jnp.float32),
            pltpu.VMEM((8, LANES), jnp.float32),
            field_type,
            power_type,
        ),
        in_specs=[VMEM] * 8,
        out_specs=(VMEM,) * 4,
        scratch_shapes=[
            *patch_scratch,
            pltpu.VMEM((plan.late * rows, plan.depth), jnp.bfloat16),
            *[pltpu.VMEM((rows + 3 * PAD, WIDE), jnp.float32)] * 4,
            *[pltpu.VMEM((rows, WIDE), jnp.float32)] * 2,
            pltpu.VMEM((plan.operand_half * rows, plan.wide), jnp.bfloat16),
            pltpu.VMEM(((plan.operand_blocks - plan.operand_half) * rows, plan.wide), jnp.bfloat16),
            pltpu.VMEM((plan.operand_blocks * plan.acc_rows, 2 * LANES), jnp.float32),
            pltpu.VMEM((plan.operand_blocks * plan.acc_rows, 2 * LANES), jnp.float32),
            pltpu.VMEM((2, -(-(rows + 1) // 8) * 8, LANES), jnp.float32),
        ],
        input_output_aliases={6: 2, 7: 3},
        compiler_params=params(
            plan.late * rows * plan.depth * 2
            + plan.operand_blocks * (rows * plan.wide * 2 + plan.acc_rows * 16 * LANES)
        ),
        cost_estimate=cost(12000),
        name="late",
    )(in_vmem(jnp.transpose(offsets)), in_vmem(load_weights[None]), own, near, far, bands, in_vmem(field), in_vmem(power))

    terms = [in_vmem(t) for t in sum_terms(sums, "gx", nx)]
    update, loss = pl.pallas_call(
        functools.partial(update_kernel, plan),
        out_shape=(
            jax.ShapeDtypeStruct((tile_rows, tile_cols), jnp.float32),
            jax.ShapeDtypeStruct((1, 1), jnp.float32),
        ),
        in_specs=[VMEM] * (2 + len(terms)),
        out_specs=(VMEM, VMEM),
        compiler_params=params(0),
        name="update",
    )(in_vmem(mask), in_vmem(grad), *terms)
    return update, loss.reshape(())


def solution(mesh):
    return jax.shard_map(
        body,
        mesh=mesh,
        in_specs=(P("gy", "gx"), P("gy", "gx"), P(), P(), P()),
        out_specs=(P("gy", "gx"), P()),
        check_vma=False,
    )
```
